256 devices in a mesh: gx: 64 (over z, y, core), gz: 4 (over x).
Axes of the slice: x: 4, y: 4, z: 8, core: 2. Of those that a mesh axis runs over, the one named last changes fastest.
Arguments:
- intensity: bfloat16 [512, 256, 512], P('gx', None, 'gz'), may hold values from 0 to 1
- membrane: bfloat16 [512, 256, 512], P('gx', None, 'gz'), may hold values from 0 to 1
- synapse: bfloat16 [512, 256, 512], P('gx', None, 'gz'), may hold values from 0 to 1
- transfer: float32 [4, 16], replicated, may hold values from 0 to 1
- occupancy: int32 [64, 32, 64], P('gx', None, 'gz'), may hold values from 0 to 1, as said below
Outputs:
- x_image: float32 [4, 256, 512], P(None, 'gx', 'gz')
- z_image: float32 [4, 512, 256], P(None, 'gx', 'gz')
The draws below stay inside these ranges and needn't reach their ends.
Inputs may be any that keep to these rules, and one draw needn't show every extreme that they name: `occupancy`: 1 marks an occupied block; every cell of a block marked 0 is empty.
All inputs are finite; a program needn't handle non-finite values.
Results may differ from the reference program's by a relative error of at most 0.0003.
Values may be sent and summed in bfloat16 or wider, within the bound.
No kernel may reach another device: no remote copies, remote signals or barrier semaphores. Data moves between devices by JAX's collectives and lax.ppermute only.
A program may use at most 64 MiB of HBM per device.

```python
import jax
import jax.numpy as jnp
from jax import lax

Y = 256
KNOTS = 16
BLOCK = 8
NX = 512
NZ = 512


def draw_occupancy(key, part):
    key = jax.random.fold_in(key, 7)
    blocks_x = NX // BLOCK
    draws = jax.random.randint(key, (blocks_x, Y // BLOCK, NZ // BLOCK), 0, 100)
    rows = jnp.arange(blocks_x, dtype=jnp.int32)[:, None, None]
    limit = 30 + 60 * rows // max(blocks_x - 1, 1)
    return (draws < limit).astype(jnp.int32)


def levels(key, extent, cuts, low, high):
    def one(dim, shards_of):
        steps = jax.random.uniform(jax.random.fold_in(jax.random.fold_in(key, 6), dim), (shards_of,), jnp.float32, low / len(cuts), high / len(cuts))
        return jnp.repeat(jnp.exp(steps), extent[dim] // shards_of).reshape((-1,) + (1,) * (len(extent) - dim - 1))

    level = one(*cuts[0])
    for cut in cuts[1:]:
        level = level * one(*cut)
    return level


def setup_inputs(seed: int = 0) -> dict:
    keys = jax.random.split(jax.random.key(seed), 6)
    return {
        "intensity": jnp.clip(1.0 * jax.random.uniform(keys[0], (NX, Y, NZ), jnp.float32) ** levels(keys[0], (NX, Y, NZ), ((0, 64), (2, 4)), -0.2, 0.2), 0.0, 1.0).astype(jnp.bfloat16),
        "membrane": jnp.clip(1.0 * jax.random.uniform(keys[1], (NX, Y, NZ), jnp.float32) ** levels(keys[1], (NX, Y, NZ), ((0, 64), (2, 4)), -0.2, 0.2), 0.0, 1.0).astype(jnp.bfloat16),
        "synapse": jnp.clip(1.0 * jax.random.uniform(keys[2], (NX, Y, NZ), jnp.float32) ** levels(keys[2], (NX, Y, NZ), ((0, 64), (2, 4)), -0.2, 0.2), 0.0, 1.0).astype(jnp.bfloat16),
        "transfer": jnp.clip(jax.random.uniform(keys[3], (4, KNOTS), jnp.float32, 0.0, 1.0), 0.0, 1.0),
        "occupancy": draw_occupancy(jax.random.fold_in(keys[5], 71), 0),
    }


MEMBRANE_COLOR = (0.9, 0.2, 0.1)
SYNAPSE_COLOR = (0.1, 0.8, 0.3)

def transfer_lookup(value, transfer):
    t_pos = jnp.clip(value, 0.0, 1.0) * (KNOTS - 1)
    outs = [jnp.zeros_like(value) for c in range(4)]
    for k in range(KNOTS):
        weight = jnp.maximum(0.0, 1.0 - jnp.abs(t_pos - k))
        for c in range(4):
            outs[c] = outs[c] + weight * transfer[c, k]
    return outs

def cell_terms(value, grad_x, grad_y, grad_z, lit, memb, syn, tables, occupied, spacing):
    norm = jnp.sqrt(grad_x * grad_x + grad_y * grad_y + grad_z * grad_z + 0.25)
    shade = 0.3 + 0.7 * jnp.abs(lit) / norm
    sigma = (tables[3] + 1.5 * memb + 0.5 * syn) * occupied
    alpha = 1.0 - jnp.exp(-sigma * spacing)
    colors = []
    for c in range(3):
        emission = shade * tables[c] + memb * MEMBRANE_COLOR[c] + syn * SYNAPSE_COLOR[c]
        colors.append(alpha * emission)
    return (jnp.stack(colors), alpha)

def reference(intensity, membrane, synapse, transfer, occupancy):

    def step(carry, xpos):
        acc, trans = carry
        xpos = xpos.astype(jnp.int32)
        center = lax.dynamic_index_in_dim(intensity, xpos, 0, False).astype(jnp.float32)
        prev = lax.dynamic_index_in_dim(intensity, jnp.maximum(xpos - 1, 0), 0, False).astype(jnp.float32)
        after = lax.dynamic_index_in_dim(intensity, jnp.minimum(xpos + 1, NX - 1), 0, False).astype(jnp.float32)
        prev = jnp.where(xpos > 0, prev, 0.0)
        after = jnp.where(xpos < NX - 1, after, 0.0)
        grad_x = 0.5 * (after - prev)
        padded = jnp.pad(center, 1)
        grad_y = 0.5 * (padded[2:, 1:-1] - padded[:-2, 1:-1])
        grad_z = 0.5 * (padded[1:-1, 2:] - padded[1:-1, :-2])
        memb = lax.dynamic_index_in_dim(membrane, xpos, 0, False).astype(jnp.float32)
        syn = lax.dynamic_index_in_dim(synapse, xpos, 0, False).astype(jnp.float32)
        blocks = lax.dynamic_index_in_dim(occupancy, xpos // BLOCK, 0, False).astype(jnp.float32)
        occupied = jnp.repeat(jnp.repeat(blocks, BLOCK, 0), BLOCK, 1)
        tables = transfer_lookup(center, transfer)
        color_x, alpha_x = cell_terms(center, grad_x, grad_y, grad_z, grad_x, memb, syn, tables, occupied, 2.0 / NX)
        acc = acc + trans[None] * color_x
        trans = trans * (1.0 - alpha_x)
        color_z, alpha_z = cell_terms(center, grad_x, grad_y, grad_z, grad_z, memb, syn, tables, occupied, 2.0 / NZ)
        keep = 1.0 - alpha_z
        running = jnp.cumprod(keep, axis=1)
        before = jnp.concatenate([jnp.ones((Y, 1), jnp.float32), running[:, :-1]], axis=1)
        rgb_z = lax.optimization_barrier(jnp.sum(color_z * before[None], axis=2))
        opac_z = 1.0 - running[:, -1]
        return ((acc, trans), jnp.concatenate([rgb_z, opac_z[None]], axis=0))
    init = (jnp.zeros((3, Y, NZ), jnp.float32), jnp.ones((Y, NZ), jnp.float32))
    (acc, trans), zrows = lax.scan(step, init, jnp.arange(NX, dtype=jnp.int32))
    x_image = jnp.concatenate([acc, (1.0 - trans)[None]], axis=0)
    z_image = jnp.transpose(zrows, (1, 0, 2))
    return (x_image, z_image)
```

```python
import jax
import jax.numpy as jnp
from jax import lax
from jax.experimental import pallas as pl
from jax.experimental.pallas import tpu as pltpu
from jax.sharding import Mesh, PartitionSpec as P

MEMBRANE_COLOR = (0.9, 0.2, 0.1)
SYNAPSE_COLOR = (0.1, 0.8, 0.3)
LX, H, LZ = 8, 256, 128
KNOTS = 16
ROWS = 64
CHIPS = 32
F32, BF16 = jnp.float32, jnp.bfloat16
CODE_SCALE = 32760.0 / 12.0
CODE_MID = 13.0
LN2 = 0.6931471805599453
NN = (((1,), (0,)), ((), ()))
NT = (((1,), (1,)), ((), ()))
TN = (((0,), (0,)), ((), ()))


def mxu(a, b, dims):
    return lax.dot_general(a, b, dims, preferred_element_type=F32)


def iota(shape, dim):
    return lax.broadcasted_iota(jnp.int32, shape, dim)


def as_bf16(mask, value=1.0):
    return jnp.where(mask, value, 0.0).astype(BF16)


def split(value):
    high = value.astype(BF16)
    return high, (value - high.astype(F32)).astype(BF16)


def faces_kernel(pos, intensity, even_x, odd_x, face_a, face_b):
    core, odd_z = pos[0], pos[1] % 2
    even_x[...] = intensity[jnp.where(core == 0, LX - 1, 0)]
    odd_x[...] = intensity[jnp.where(core == 0, 0, LX - 1)]
    row, lane = iota((16, LZ), 0), iota((16, LZ), 1)
    lane_a = jnp.where(odd_z == 0, LZ - 1, 0)
    wanted = jnp.where(row < LX, lane_a, LZ - 1 - lane_a)
    total = jnp.zeros((16, H), F32)
    for x in range(LX):
        pick = as_bf16((row % LX == x) & (lane == wanted))
        total = total + mxu(pick, intensity[x], NT)
    face_a[...] = total[:LX]
    face_b[...] = total[LX:]


def brick_kernel(
    pos, inten, memb, syn, transfer, occ, even_x, odd_x, face_a, face_b,
    keep, send, z0, z1, z2, z3,
    pad, halo, table, occ_rows, dy, dz, prefix, depth, parts, zsum,
):
    core, zpos = pos[0], pos[1]
    odd_z = zpos % 2
    zero = jnp.zeros((16, LZ), BF16)
    for x in range(LX + 2):
        pad[x, 0:16, :] = zero
        pad[x, 16 + H :, :] = zero
    low = jnp.where(core == 0, odd_x[...].astype(F32), even_x[...].astype(F32))
    high = jnp.where(core == 0, even_x[...].astype(F32), odd_x[...].astype(F32))
    pad[0, 16 : 16 + H, :] = low.astype(BF16)
    pad[LX + 1, 16 : 16 + H, :] = high.astype(BF16)
    for x in range(LX):
        pad[x + 1, 16 : 16 + H, :] = inten[x]
    near = jnp.where(odd_z == 0, face_b[...], face_a[...])
    far = jnp.where(odd_z == 0, face_a[...], face_b[...])
    both = jnp.concatenate([near, far], axis=0).astype(BF16)
    halo[...] = mxu(both, as_bf16(iota((16, LZ), 0) == iota((16, LZ), 1)), TN).astype(BF16)
    table[...] = jnp.zeros((8, LZ), F32)
    table[0:4, 0:KNOTS] = transfer[...]
    spread = as_bf16(iota((KNOTS, LZ), 1) // 8 == iota((KNOTS, LZ), 0))
    occ_rows[...] = mxu(occ[0].astype(F32).astype(BF16), spread, NN)

    knots = table[...]
    steps = pltpu.roll(knots, LZ - 1, 1) - knots
    scale = 2.0 / (LX * 64)
    firsts, slopes = [], []
    for c in range(4):
        factor = scale if c == 3 else 1.0
        firsts.append(jnp.broadcast_to(knots[c : c + 1], (16, LZ)) * factor)
        slopes.append(jnp.broadcast_to(steps[c : c + 1], (16, LZ)) * factor)

    k, n = iota((2 * LZ, LZ), 0), iota((2 * LZ, LZ), 1)
    up = ((k < LZ) & (k == n + 1)) | ((k >= LZ + LX) & (k < LZ + 2 * LX) & (n == LZ - 1))
    down = ((k < LZ) & (k == n - 1)) | ((k >= LZ) & (k < LZ + LX) & (n == 0))
    diff_z = (jnp.where(up, 1.0, 0.0) - jnp.where(down, 1.0, 0.0)).astype(BF16)
    before = as_bf16(k % LZ < n)
    r, k2 = iota((ROWS, ROWS + 32), 0), iota((ROWS, ROWS + 32), 1)
    diff_y = (jnp.where(k2 == r + 17, 1.0, 0.0) - jnp.where(k2 == r + 15, 1.0, 0.0)).astype(BF16)
    lanes = iota((ROWS, LZ), 1)
    ones_row = iota((8, 2 * LZ), 0)

    def lookup(value):
        t = jnp.clip(value, 0.0, 1.0) * (KNOTS - 1.0)
        index = jnp.minimum(t.astype(jnp.int32), KNOTS - 2)
        return index, t - index.astype(F32)

    def interpolate(c, index, frac):
        first = jnp.take_along_axis(firsts[c], index, axis=1)
        return first + frac * jnp.take_along_axis(slopes[c], index, axis=1)

    def chunk(j, carry):
        base = pl.multiple_of(j * ROWS, ROWS)
        halo_rows = halo[pl.ds(base, ROWS), :]
        for x in range(LX):
            rows = pl.ds(pl.multiple_of(base + 16, 16), ROWS)
            mine = jnp.where((lanes == x) | (lanes == LX + x), halo_rows, jnp.zeros_like(halo_rows))
            left = jnp.concatenate([pad[x + 1, rows, :], mine], axis=1)
            dz[x] = mxu(left, diff_z, NN)
            dy[x] = mxu(diff_y, pad[x + 1, pl.ds(base, ROWS + 32), :], NN)
        for x in range(LX):
            for b in range(0, ROWS, 16):
                rows = pl.ds(pl.multiple_of(base + b, 16), 16)
                value = pad[x + 1, pl.ds(pl.multiple_of(base + 16 + b, 16), 16), :].astype(F32)
                index, frac = lookup(value)
                sigma = interpolate(3, index, frac)
                sigma = sigma + memb[x, rows, :].astype(F32) * (1.5 * scale)
                sigma = sigma + syn[x, rows, :].astype(F32) * (0.5 * scale)
                block = pl.ds(base // 8 + b // 8, 2)
                mask = occ_rows[block, :]
                mask = jnp.concatenate(
                    [jnp.broadcast_to(mask[0:1], (8, LZ)), jnp.broadcast_to(mask[1:2], (8, LZ))], axis=0
                )
                sigma = sigma * mask
                depth[x, b : b + 16, :] = sigma
                high, low = split(sigma)
                parts[3, x * ROWS + b : x * ROWS + b + 16, 0:LZ] = high
                parts[3, x * ROWS + b : x * ROWS + b + 16, LZ:] = low
        prefix[...] = mxu(parts[3], before, NN)
        for b in range(0, ROWS, 16):
            rows = pl.ds(pl.multiple_of(base + b, 16), 16)
            trans = jnp.ones((16, LZ), F32)
            total = jnp.zeros((16, LZ), F32)
            acc = [jnp.zeros((16, LZ), F32) for c in range(3)]
            for x in range(LX):
                here = pl.ds(pl.multiple_of(base + 16 + b, 16), 16)
                value = pad[x + 1, here, :].astype(F32)
                grad_x = pad[x + 2, here, :].astype(F32) - pad[x, here, :].astype(F32)
                grad_y, grad_z = dy[x, b : b + 16, :], dz[x, b : b + 16, :]
                norm = lax.rsqrt(grad_x * grad_x + grad_y * grad_y + grad_z * grad_z + 1.0) * 0.7
                shade_x = 0.3 + jnp.abs(grad_x) * norm
                shade_z = 0.3 + jnp.abs(grad_z) * norm
                sigma = depth[x, b : b + 16, :]
                passed = jnp.exp(-sigma)
                alpha = 1.0 - passed
                weight_x = trans * alpha
                trans = trans * passed
                total = total + sigma
                row = x * ROWS + b
                weight_z = jnp.exp(-prefix[row : row + 16, :]) * alpha
                index, frac = lookup(value)
                mem = memb[x, rows, :].astype(F32)
                sy = syn[x, rows, :].astype(F32)
                for c in range(3):
                    color = interpolate(c, index, frac)
                    own = mem * MEMBRANE_COLOR[c] + sy * SYNAPSE_COLOR[c]
                    acc[c] = acc[c] + weight_x * (shade_x * color + own)
                    high, low = split(weight_z * (shade_z * color + own))
                    parts[c, row : row + 16, 0:LZ] = high
                    parts[c, row : row + 16, LZ:] = low
            first_half = iota((8, LZ), 0) < 4
            for s in range(2):
                a, d, g, t = [v[8 * s : 8 * s + 8] for v in (*acc, total)]
                swap = lambda v: pltpu.roll(v, 4, 0)
                for_0 = (jnp.where(first_half, a, swap(d)), jnp.where(first_half, g, swap(t)))
                for_1 = (jnp.where(first_half, swap(a), d), jnp.where(first_half, swap(g), t))
                chip = base // 8 + b // 8 + s
                for i in range(2):
                    keep[chip, 8 * i : 8 * i + 8, :] = jnp.where(core == 0, for_0[i], for_1[i])
                    send[chip, 8 * i : 8 * i + 8, :] = jnp.where(core == 0, for_1[i], for_0[i])
        sums = jnp.zeros((8, LX * ROWS), F32)
        for c in range(4):
            sums = sums + mxu(as_bf16(ones_row == c), parts[c], NT)
        zsum[j] = sums
        return carry

    lax.fori_loop(0, H // ROWS, chunk, 0)
    for i, out in enumerate((z0, z1, z2, z3)):
        out[...] = zsum[zpos ^ i]


def depth_rows(b):
    return jnp.where(iota((8, LZ), 0) < 4, pltpu.roll(b, 4, 0), b)


def pair_kernel(pos, mine, other, code):
    core = pos[0]
    first_half = iota((8, LZ), 0) < 4

    def chip(i, carry):
        ma, mb = mine[i, 0:8, :], mine[i, 8:16, :]
        oa, ob = other[i, 0:8, :], other[i, 8:16, :]
        fa, fb = jnp.where(core == 0, ma, oa), jnp.where(core == 0, mb, ob)
        sa, sb = jnp.where(core == 0, oa, ma), jnp.where(core == 0, ob, mb)
        passed = jnp.exp(-depth_rows(fb))
        a = fa + passed * sa
        b = fb + jnp.where(first_half, passed, 1.0) * sb
        v = jnp.concatenate([a, b], axis=0)
        q = (jnp.log(jnp.maximum(v, 2.0**-25)) * (1.0 / LN2) + CODE_MID) * CODE_SCALE
        q = jnp.where(v > 2.0**-25, jnp.round(jnp.clip(q, -32766.0, 32766.0)), -32768.0)
        code[i] = q.astype(jnp.int32).astype(jnp.int16)
        return carry

    lax.fori_loop(0, CHIPS, chip, 0, unroll=4)


def final_kernel(pos, code, z0, z1, z2, z3, x_image, z_image, decoded):
    zpos = pos[1]

    def decode(i, carry):
        q = code[i].astype(F32)
        v = jnp.exp(q * (LN2 / CODE_SCALE) - CODE_MID * LN2)
        decoded[i] = jnp.where(q < -32767.0, 0.0, v)
        return carry

    lax.fori_loop(0, CHIPS, decode, 0, unroll=4)

    def chip(i, carry):
        a, b, deep = carry
        passed = jnp.exp(-deep)
        here = decoded[i, 8:16, :]
        return (a + passed * decoded[i, 0:8, :], b + passed * here, deep + depth_rows(here))

    empty = jnp.zeros((8, LZ), F32)
    a, b, deep = lax.fori_loop(0, CHIPS, chip, (empty, empty, empty), unroll=4)
    x_image[0] = a[0:4]
    x_image[1] = a[4:8]
    x_image[2] = b[0:4]
    x_image[3] = (1.0 - jnp.exp(-deep))[0:4]

    shape = (8, LX * ROWS)
    terms = [z[...] for z in (z0, z1, z2, z3)]
    depths = [jnp.broadcast_to(t[3:4], shape) for t in terms]
    image = jnp.zeros(shape, F32)
    whole = jnp.zeros(shape, F32)
    for i in range(4):
        ahead = jnp.zeros(shape, F32)
        for m in range(4):
            if m != i:
                ahead = ahead + jnp.where((zpos ^ m) < (zpos ^ i), depths[m], 0.0)
        image = image + jnp.exp(-ahead) * terms[i]
        whole = whole + depths[i]
    image = jnp.where(iota(shape, 0) == 3, 1.0 - jnp.exp(-whole), image)
    for x in range(LX):
        z_image[:, x, :] = image[0:4, x * ROWS : (x + 1) * ROWS]


def call(kernel, out_shape, scratch, cost, *operands):
    specs = [pl.BlockSpec(memory_space=pltpu.SMEM)] + [pl.BlockSpec(memory_space=pltpu.VMEM)] * (len(operands) - 1)
    return pl.pallas_call(
        kernel,
        out_shape=out_shape,
        in_specs=specs,
        out_specs=[pl.BlockSpec(memory_space=pltpu.VMEM)] * len(out_shape),
        scratch_shapes=scratch,
        compiler_params=pltpu.CompilerParams(vmem_limit_bytes=40 * 2**20),
        cost_estimate=pl.CostEstimate(flops=cost, bytes_accessed=2**20, transcendentals=0),
    )(*operands)


def body(intensity, membrane, synapse, transfer, occupancy):
    shape = jax.ShapeDtypeStruct
    core, zpos = lax.axis_index("core"), lax.axis_index("x")
    pos = jnp.stack([core, zpos]).astype(jnp.int32)
    layer, face = shape((H, LZ), BF16), shape((LX, H), F32)
    even_x, odd_x, face_a, face_b = call(
        faces_kernel, [layer, layer, face, face], [], 10**6, pos, intensity
    )
    gx = ("z", "y", "core")
    even = [p for i in range(0, 64, 2) for p in ((i, i + 1), (i + 1, i))]
    odd = [p for i in range(1, 63, 2) for p in ((i, i + 1), (i + 1, i))]
    odd_x = lax.ppermute(odd_x, gx, odd)
    face_a = lax.ppermute(face_a, "x", [(0, 1), (1, 0), (2, 3), (3, 2)])
    face_b = lax.ppermute(face_b, "x", [(1, 2), (2, 1)])
    even_x = lax.ppermute(even_x, gx, even)
    half = shape((CHIPS, 16, LZ), F32)
    zpart = shape((8, LX * ROWS), F32)
    scratch = [
        pltpu.VMEM((LX + 2, H + 32, LZ), BF16),
        pltpu.VMEM((H, LZ), BF16),
        pltpu.VMEM((8, LZ), F32),
        pltpu.VMEM((H // 8, LZ), F32),
        pltpu.VMEM((LX, ROWS, LZ), F32),
        pltpu.VMEM((LX, ROWS, LZ), F32),
        pltpu.VMEM((LX * ROWS, LZ), F32),
        pltpu.VMEM((LX, ROWS, LZ), F32),
        pltpu.VMEM((4, LX * ROWS, 2 * LZ), BF16),
        pltpu.VMEM((H // ROWS, 8, LX * ROWS), F32),
    ]
    keep, send, *zs = call(
        brick_kernel, [half, half] + [zpart] * 4, scratch, 10**8,
        pos, intensity, membrane, synapse, transfer, occupancy, even_x, odd_x, face_a, face_b,
    )
    other = lax.ppermute(send, "core", [(0, 1), (1, 0)])
    for i in range(1, 4):
        zs[i] = lax.ppermute(zs[i], "x", [(d, d ^ i) for d in range(4)])
    (code,) = call(pair_kernel, [shape((CHIPS, 16, LZ), jnp.int16)], [], 10**6, pos, keep, other)
    code = lax.all_to_all(code, ("z", "y"), split_axis=0, concat_axis=0, tiled=True)
    images = [shape((4, 4, LZ), F32), shape((4, LX, ROWS), F32)]
    scratch = [pltpu.VMEM((CHIPS, 16, LZ), F32)]
    return tuple(call(final_kernel, images, scratch, 10**6, pos, code, *zs))


def solution(mesh):
    split_mesh = Mesh(mesh.devices.reshape(8, 4, 2, 4), ("z", "y", "core", "x"))
    gx = ("z", "y", "core")
    brick = P(gx, None, "x")
    return jax.shard_map(
        body,
        mesh=split_mesh,
        in_specs=(brick, brick, brick, P(), brick),
        out_specs=(P(None, gx, "x"), P(None, gx, "x")),
        check_vma=False,
    )
```

```python
import jax
import jax.numpy as jnp
from jax import lax
from jax.experimental import pallas as pl
from jax.experimental.pallas import tpu as pltpu
from jax.sharding import Mesh, PartitionSpec as P

MEMBRANE_COLOR = (0.9, 0.2, 0.1)
SYNAPSE_COLOR = (0.1, 0.8, 0.3)
LX, H, LZ = 8, 256, 128
KNOTS = 16
ROWS = 64
CHIPS = 32
WIDE = 52 * 2**20
F32, BF16 = jnp.float32, jnp.bfloat16
CODE_SCALE = 32760.0 / 12.0
CODE_MID = 13.0
LN2 = 0.6931471805599453
NN = (((1,), (0,)), ((), ()))
NT = (((1,), (1,)), ((), ()))
TN = (((0,), (0,)), ((), ()))


def mxu(a, b, dims):
    return lax.dot_general(a, b, dims, preferred_element_type=F32)


def iota(shape, dim):
    return lax.broadcasted_iota(jnp.int32, shape, dim)


def as_bf16(mask, value=1.0):
    return jnp.where(mask, value, 0.0).astype(BF16)


def split(value):
    high = value.astype(BF16)
    return high, (value - high.astype(F32)).astype(BF16)


def faces_kernel(
    pos, inten_hbm, memb_hbm, syn_hbm, transfer_hbm,
    even_x, odd_x, face_a, face_b, intensity, memb, syn, transfer, sems,
):
    pairs = ((inten_hbm, intensity), (memb_hbm, memb), (syn_hbm, syn), (transfer_hbm, transfer))
    copies = [pltpu.make_async_copy(a, b, sems.at[i]) for i, (a, b) in enumerate(pairs)]
    for copy in copies:
        copy.start()
    copies[0].wait()
    core, odd_z = pos[0], pos[1] % 2
    even_x[...] = intensity[jnp.where(core == 0, LX - 1, 0)]
    odd_x[...] = intensity[jnp.where(core == 0, 0, LX - 1)]
    row, lane = iota((16, LZ), 0), iota((16, LZ), 1)
    lane_a = jnp.where(odd_z == 0, LZ - 1, 0)
    wanted = jnp.where(row < LX, lane_a, LZ - 1 - lane_a)
    total = jnp.zeros((16, H), F32)
    for x in range(LX):
        pick = as_bf16((row % LX == x) & (lane == wanted))
        total = total + mxu(pick, intensity[x], NT)
    face_a[...] = total[:LX]
    face_b[...] = total[LX:]
    for copy in copies[1:]:
        copy.wait()


def lookup(value):
    t = jnp.clip(value, 0.0, 1.0) * (KNOTS - 1.0)
    index = jnp.minimum(t.astype(jnp.int32), KNOTS - 2)
    return index, t - index.astype(F32)


def gather(table, index):
    numbers = lax.GatherDimensionNumbers(
        offset_dims=(), collapsed_slice_dims=(1,), start_index_map=(1,),
        operand_batching_dims=(0,), start_indices_batching_dims=(0,),
    )
    return lax.gather(
        table, index[..., None], numbers, (1, 1), mode=lax.GatherScatterMode.PROMISE_IN_BOUNDS
    )


def knot_tables(transfer, table, channels, factor):
    table[...] = jnp.zeros((8, LZ), F32)
    table[0:4, 0:KNOTS] = transfer[...] * factor
    knots = table[...]
    steps = pltpu.roll(knots, LZ - 1, 1) - knots
    return [
        (jnp.broadcast_to(knots[c : c + 1], (16, LZ)), jnp.broadcast_to(steps[c : c + 1], (16, LZ)))
        for c in channels
    ]


def interpolate(pair, index, frac):
    return gather(pair[0], index) + frac * gather(pair[1], index)


def depth_kernel(
    inten, memb, syn, transfer, occ,
    weight_x, weight_z, steep, spot, along, total_x, total_z,
    table, occ_rows, sigma, parts,
):
    scale = -2.0 / (LX * 64) / LN2
    (knots,) = knot_tables(transfer, table, (3,), scale)
    spread = as_bf16(iota((KNOTS, LZ), 1) // 8 == iota((KNOTS, LZ), 0))
    occ_rows[...] = mxu(occ[0].astype(F32).astype(BF16), spread, NN)
    r, k = iota((H, H), 0), iota((H, H), 1)
    diff_y = (jnp.where(k == r + 1, 1.0, 0.0) - jnp.where(k == r - 1, 1.0, 0.0)).astype(BF16)
    k, n = iota((2 * LZ, LZ), 0), iota((2 * LZ, LZ), 1)
    before = as_bf16(k % LZ < n)
    ones = jnp.ones((8, 2 * LZ), BF16)
    for x in range(LX):
        grad_y = mxu(diff_y, inten[x], NN)
        steep[x] = grad_y * grad_y + 1.0
    for j in range(H // ROWS):
        buf = j % 2
        for b in range(0, ROWS, 16):
            rows = pl.ds(j * ROWS + b, 16)
            block = (j * ROWS + b) // 8
            mask = jnp.concatenate(
                [jnp.broadcast_to(occ_rows[block + i : block + i + 1, :], (8, LZ)) for i in range(2)], axis=0
            )
            total = jnp.zeros((16, LZ), F32)
            trans = jnp.ones((16, LZ), F32)
            for x in range(LX):
                index, frac = lookup(inten[x, rows, :].astype(F32))
                spot[x, rows, :] = index
                along[x, rows, :] = frac
                depth = interpolate(knots, index, frac)
                depth = depth + memb[x, rows, :].astype(F32) * (1.5 * scale)
                depth = (depth + syn[x, rows, :].astype(F32) * (0.5 * scale)) * mask
                high, low = split(depth)
                row = x * ROWS + b
                parts[buf, row : row + 16, 0:LZ] = high
                parts[buf, row : row + 16, LZ:] = low
                passed = jnp.exp2(depth)
                alpha = 1.0 - passed
                sigma[buf, row : row + 16, :] = alpha
                weight_x[x, rows, :] = trans * alpha
                trans = trans * passed
                total = total + depth
            total_x[rows, :] = total
        prefix = mxu(parts[buf], before, NN)
        for x in range(LX):
            here = slice(x * ROWS, x * ROWS + ROWS)
            weight_z[x, j * ROWS : (j + 1) * ROWS, :] = jnp.exp2(prefix[here]) * sigma[buf, here, :]
        total_z[j] = mxu(ones, parts[buf], NT)


def shade_kernel(
    pos, inten, memb, syn, transfer, weight_x, weight_z, steep, spot, along, total_x, total_z,
    even_x, odd_x, face_a, face_b,
    keep, send, z_keep, z_send,
    pad, halo, table, left, dz, parts, zsum,
):
    core, zpos = pos[0], pos[1]
    odd_z = zpos % 2
    gx = pos[2]
    low = jnp.where(core == 0, odd_x[...].astype(F32), even_x[...].astype(F32))
    high = jnp.where(core == 0, even_x[...].astype(F32), odd_x[...].astype(F32))
    pad[0] = jnp.where(gx == 0, 0.0, low)
    pad[1] = jnp.where(gx == 63, 0.0, high)
    near = jnp.where(zpos == 0, 0.0, jnp.where(odd_z == 0, face_b[...], face_a[...]))
    far = jnp.where(zpos == 3, 0.0, jnp.where(odd_z == 0, face_a[...], face_b[...]))
    both = jnp.concatenate([near, far], axis=0).astype(BF16)
    halo[...] = mxu(both, as_bf16(iota((16, LZ), 0) == iota((16, LZ), 1)), TN).astype(BF16)
    knots = knot_tables(transfer, table, (0, 1, 2), 1.0)
    k, n = iota((2 * LZ, LZ), 0), iota((2 * LZ, LZ), 1)
    up = ((k < LZ) & (k == n + 1)) | ((k >= LZ + LX) & (k < LZ + 2 * LX) & (n == LZ - 1))
    down = ((k < LZ) & (k == n - 1)) | ((k >= LZ) & (k < LZ + LX) & (n == 0))
    diff_z = (jnp.where(up, 1.0, 0.0) - jnp.where(down, 1.0, 0.0)).astype(BF16)
    lanes = iota((ROWS, LZ), 1)
    ones_row = iota((8, 2 * LZ), 0)
    first_half = iota((8, LZ), 0) < 4

    for j in range(H // ROWS):
        buf = j % 2
        base = j * ROWS
        halo_rows = halo[base : base + ROWS, :]
        for x in range(LX):
            mine = jnp.where((lanes == x) | (lanes == LX + x), halo_rows, jnp.zeros_like(halo_rows))
            left[buf, x * ROWS : (x + 1) * ROWS, 0:LZ] = inten[x, base : base + ROWS, :]
            left[buf, x * ROWS : (x + 1) * ROWS, LZ:] = mine
        dz[buf] = mxu(left[buf], diff_z, NN)
        for b in range(0, ROWS, 16):
            rows = pl.ds(base + b, 16)
            acc = [jnp.zeros((16, LZ), F32) for c in range(3)]
            values = [pad[0, rows, :]] + [inten[x, rows, :].astype(F32) for x in range(LX)] + [pad[1, rows, :]]
            for x in range(LX):
                row = x * ROWS + b
                grad_x = values[x + 2] - values[x]
                grad_z = dz[buf, row : row + 16, :]
                norm = lax.rsqrt(grad_x * grad_x + (grad_z * grad_z + steep[x, rows, :])) * 0.7
                shade_x = 0.3 + jnp.abs(grad_x) * norm
                shade_z = 0.3 + jnp.abs(grad_z) * norm
                wx, wz = weight_x[x, rows, :], weight_z[x, rows, :]
                index, frac = spot[x, rows, :], along[x, rows, :]
                mem = memb[x, rows, :].astype(F32)
                sy = syn[x, rows, :].astype(F32)
                for c in range(3):
                    color = interpolate(knots[c], index, frac)
                    own = mem * MEMBRANE_COLOR[c] + sy * SYNAPSE_COLOR[c]
                    acc[c] = acc[c] + wx * (shade_x * color + own)
                    high, low = split(wz * (shade_z * color + own))
                    parts[buf, c, row : row + 16, 0:LZ] = high
                    parts[buf, c, row : row + 16, LZ:] = low
            total = -total_x[rows, :]
            for s in range(2):
                a, d, g, t = [v[8 * s : 8 * s + 8] for v in (*acc, total)]
                swap = lambda v: pltpu.roll(v, 4, 0)
                for_0 = (jnp.where(first_half, a, swap(d)), jnp.where(first_half, g, swap(t)))
                for_1 = (jnp.where(first_half, swap(a), d), jnp.where(first_half, swap(g), t))
                chip = (base + b) // 8 + s
                for i in range(2):
                    keep[chip, 8 * i : 8 * i + 8, :] = jnp.where(core == 0, for_0[i], for_1[i])
                    send[chip, 8 * i : 8 * i + 8, :] = jnp.where(core == 0, for_1[i], for_0[i])
        sums = jnp.where(iota((8, LX * ROWS), 0) % 4 == 3, -total_z[j], 0.0)
        for c in range(3):
            sums = sums + mxu(as_bf16(ones_row % 4 == c), parts[buf, c], NT)
        zsum[j] = sums
    for out, chip in ((z_keep, zpos), (z_send, zpos ^ 1)):
        out[...] = jnp.where(iota((8, LX * ROWS), 0) < 4, zsum[chip], zsum[3 - chip])


def depth_rows(b):
    return jnp.where(iota((8, LZ), 0) < 4, pltpu.roll(b, 4, 0), b)


def z_rows(z):
    upper = iota(z.shape, 0) < 4
    return jnp.where(upper, jnp.broadcast_to(z[3:4], z.shape), jnp.broadcast_to(z[7:8], z.shape))


def z_merge(first, second):
    depth_row = iota(first.shape, 0) % 4 == 3
    return first + jnp.where(depth_row, 1.0, jnp.exp2(-z_rows(first))) * second


def pair_kernel(pos, mine, other, z_mine, z_other, code, z_pair):
    core = pos[0]
    even = pos[1] % 2 == 0
    zm, zo = z_mine[...], z_other[...]
    z_pair[...] = z_merge(jnp.where(even, zm, zo), jnp.where(even, zo, zm))
    first_half = iota((8, LZ), 0) < 4
    for i in range(CHIPS):
        ma, mb = mine[i, 0:8, :], mine[i, 8:16, :]
        oa, ob = other[i, 0:8, :], other[i, 8:16, :]
        fa, fb = jnp.where(core == 0, ma, oa), jnp.where(core == 0, mb, ob)
        sa, sb = jnp.where(core == 0, oa, ma), jnp.where(core == 0, ob, mb)
        passed = jnp.exp2(-depth_rows(fb))
        a = fa + passed * sa
        b = fb + jnp.where(first_half, passed, 1.0) * sb
        v = jnp.concatenate([a, b], axis=0)
        q = jnp.log2(jnp.maximum(v, 2.0**-25)) * CODE_SCALE + (CODE_MID * CODE_SCALE)
        q = jnp.where(v > 2.0**-25, jnp.round(jnp.minimum(q, 32766.0)), -32768.0)
        code[i] = q.astype(jnp.int32).astype(jnp.int16)


def final_kernel(pos, code, z_mine, z_other, x_image, z_image):
    front = pos[1] < 2
    a = b = deep = jnp.zeros((8, LZ), F32)
    for i in range(CHIPS):
        q = code[i].astype(F32)
        v = jnp.exp2(q * (1.0 / CODE_SCALE) - CODE_MID)
        v = jnp.where(q < -32767.0, 0.0, v)
        passed = jnp.exp2(-deep)
        a = a + passed * v[0:8]
        b = b + passed * v[8:16]
        deep = deep + depth_rows(v[8:16])
    x_image[0] = a[0:4]
    x_image[1] = a[4:8]
    x_image[2] = b[0:4]
    x_image[3] = (1.0 - jnp.exp2(-deep))[0:4]

    zm, zo = z_mine[...], pltpu.roll(z_other[...], 4, 0)
    image = z_merge(jnp.where(front, zm, zo), jnp.where(front, zo, zm))
    image = jnp.where(iota(image.shape, 0) == 3, 1.0 - jnp.exp2(-image), image)
    for x in range(LX):
        z_image[:, x, :] = image[0:4, x * ROWS : (x + 1) * ROWS]


def call(kernel, out_shape, scratch, cost, *operands, wide=False):
    specs = [
        pl.BlockSpec(memory_space=pltpu.SMEM if a.shape == (3,) else pl.ANY if wide else pltpu.VMEM)
        for a in operands
    ]
    return pl.pallas_call(
        kernel,
        out_shape=out_shape,
        in_specs=specs,
        out_specs=[pl.BlockSpec(memory_space=pltpu.VMEM)] * len(out_shape),
        scratch_shapes=scratch,
        compiler_params=pltpu.CompilerParams(vmem_limit_bytes=WIDE if wide else 32 * 2**20),
        cost_estimate=pl.CostEstimate(flops=cost, bytes_accessed=2**20, transcendentals=0),
    )(*operands)


LAYER, FACE = jax.ShapeDtypeStruct((H, LZ), BF16), jax.ShapeDtypeStruct((LX, H), F32)
BRICK = jax.ShapeDtypeStruct((LX, H, LZ), F32)
HALF = jax.ShapeDtypeStruct((CHIPS, 16, LZ), F32)
ZPART = jax.ShapeDtypeStruct((8, LX * ROWS), F32)
IMAGES = [jax.ShapeDtypeStruct((4, 4, LZ), F32), jax.ShapeDtypeStruct((4, LX, ROWS), F32)]
CODE = jax.ShapeDtypeStruct((CHIPS, 16, LZ), jnp.int16)


def faces(*operands):
    brick = jax.ShapeDtypeStruct((LX, H, LZ), BF16)
    outs = [LAYER, LAYER, FACE, FACE, brick, brick, brick, jax.ShapeDtypeStruct((4, KNOTS), F32)]
    return call(faces_kernel, outs, [pltpu.SemaphoreType.DMA((4,))], 10**6, *operands, wide=True)


def depths(intensity, membrane, synapse, transfer, occupancy):
    outs = [BRICK] * 3 + [jax.ShapeDtypeStruct((LX, H, LZ), jnp.int32), BRICK] + [
        jax.ShapeDtypeStruct((H, LZ), F32),
        jax.ShapeDtypeStruct((H // ROWS, 8, LX * ROWS), F32),
    ]
    scratch = [
        pltpu.VMEM((8, LZ), F32),
        pltpu.VMEM((H // 8, LZ), F32),
        pltpu.VMEM((2, LX * ROWS, LZ), F32),
        pltpu.VMEM((2, LX * ROWS, 2 * LZ), BF16),
    ]
    return call(depth_kernel, outs, scratch, 10**8, intensity, membrane, synapse, transfer, occupancy)


def shades(*operands):
    scratch = [
        pltpu.VMEM((2, H, LZ), F32),
        pltpu.VMEM((H, LZ), BF16),
        pltpu.VMEM((8, LZ), F32),
        pltpu.VMEM((2, LX * ROWS, 2 * LZ), BF16),
        pltpu.VMEM((2, LX * ROWS, LZ), F32),
        pltpu.VMEM((2, 3, LX * ROWS, 2 * LZ), BF16),
        pltpu.VMEM((H // ROWS, 8, LX * ROWS), F32),
    ]
    return call(shade_kernel, [HALF, HALF, ZPART, ZPART], scratch, 10**8, *operands)


def body(intensity, membrane, synapse, transfer, occupancy):
    gx = ("z", "y", "core")
    pos = jnp.stack([lax.axis_index("core"), lax.axis_index("x"), lax.axis_index(gx)]).astype(jnp.int32)
    even_x, odd_x, face_a, face_b, intensity, membrane, synapse, transfer = faces(
        pos, intensity, membrane, synapse, transfer
    )
    even = [p for i in range(0, 64, 2) for p in ((i, i + 1), (i + 1, i))]
    odd = [p for i in range(1, 64, 2) for p in ((i, (i + 1) % 64), ((i + 1) % 64, i))]
    odd_x = lax.ppermute(odd_x, gx, odd)
    face_a = lax.ppermute(face_a, "x", [(0, 1), (1, 0), (2, 3), (3, 2)])
    face_b = lax.ppermute(face_b, "x", [(1, 2), (2, 1), (3, 0), (0, 3)])
    even_x = lax.ppermute(even_x, gx, even)
    deep = depths(intensity, membrane, synapse, transfer, occupancy)
    keep, send, z_keep, z_send = shades(
        pos, intensity, membrane, synapse, transfer, *deep, even_x, odd_x, face_a, face_b
    )
    other = lax.ppermute(send, "core", [(0, 1), (1, 0)])
    z_other = lax.ppermute(z_send, "x", [(0, 1), (1, 0), (2, 3), (3, 2)])
    code, z_pair = call(pair_kernel, [CODE, ZPART], [], 10**6, pos, keep, other, z_keep, z_other)
    z_other = lax.ppermute(z_pair, "x", [(0, 3), (3, 0), (1, 2), (2, 1)])
    code = lax.all_to_all(code, ("z", "y"), split_axis=0, concat_axis=0, tiled=True)
    return tuple(call(final_kernel, IMAGES, [], 10**6, pos, code, z_pair, z_other))


def solution(mesh):
    split_mesh = Mesh(mesh.devices.reshape(8, 4, 2, 4), ("z", "y", "core", "x"))
    gx = ("z", "y", "core")
    brick = P(gx, None, "x")
    return jax.shard_map(
        body,
        mesh=split_mesh,
        in_specs=(brick, brick, brick, P(), brick),
        out_specs=(P(None, gx, "x"), P(None, gx, "x")),
        check_vma=False,
    )
```

```python
import jax
import jax.numpy as jnp
from jax import lax
from jax.experimental import pallas as pl
from jax.experimental.pallas import tpu as pltpu
from jax.sharding import Mesh, PartitionSpec as P

MEMBRANE_COLOR = (0.9, 0.2, 0.1)
SYNAPSE_COLOR = (0.1, 0.8, 0.3)
LX, H, LZ = 8, 256, 128
KNOTS = 16
ROWS = 64
CHIPS = 32
ACROSS = ()
WIDE = 52 * 2**20
F32, BF16 = jnp.float32, jnp.bfloat16
CODE_SCALE = 32760.0 / 12.0
CODE_MID = 13.0
LN2 = 0.6931471805599453
NN = (((1,), (0,)), ((), ()))
NT = (((1,), (1,)), ((), ()))
TN = (((0,), (0,)), ((), ()))


def mxu(a, b, dims):
    return lax.dot_general(a, b, dims, preferred_element_type=F32)


def iota(shape, dim):
    return lax.broadcasted_iota(jnp.int32, shape, dim)


def as_bf16(mask, value=1.0):
    return jnp.where(mask, value, 0.0).astype(BF16)


def split(value):
    high = value.astype(BF16)
    return high, (value - high.astype(F32)).astype(BF16)


def faces_kernel(
    pos, inten_hbm, memb_hbm, syn_hbm,
    odd_x, face_a, face_b, even_x, intensity, memb, syn, sems,
):
    pairs = ((inten_hbm, intensity), (memb_hbm, memb), (syn_hbm, syn))
    copies = [pltpu.make_async_copy(a, b, sems.at[i]) for i, (a, b) in enumerate(pairs)]
    for copy in copies:
        copy.start()
    copies[0].wait()
    core, odd_z = pos[0], pos[1] % 2
    even_x[...] = intensity[jnp.where(core == 0, LX - 1, 0)]
    odd_x[...] = intensity[jnp.where(core == 0, 0, LX - 1)]
    row, lane = iota((16, LZ), 0), iota((16, LZ), 1)
    lane_a = jnp.where(odd_z == 0, LZ - 1, 0)
    wanted = jnp.where(row < LX, lane_a, LZ - 1 - lane_a)
    total = jnp.zeros((16, H), F32)
    for x in range(LX):
        pick = as_bf16((row % LX == x) & (lane == wanted))
        total = total + mxu(pick, intensity[x], NT)
    face_a[...] = total[:LX]
    face_b[...] = total[LX:]
    for copy in copies[1:]:
        copy.wait()


def lookup(value):
    t = jnp.clip(value, 0.0, 1.0) * (KNOTS - 1.0)
    index = jnp.minimum(t.astype(jnp.int32), KNOTS - 2)
    return index, t - index.astype(F32)


def gather(table, index, dim):
    numbers = lax.GatherDimensionNumbers(
        offset_dims=(), collapsed_slice_dims=(dim,), start_index_map=(dim,),
        operand_batching_dims=(1 - dim,), start_indices_batching_dims=(1 - dim,),
    )
    return lax.gather(
        table, index[..., None], numbers, (1, 1), mode=lax.GatherScatterMode.PROMISE_IN_BOUNDS
    )


def knot_table(transfer, channel, factor, across):
    knots = transfer[...] * factor
    steps = pltpu.roll(knots, LZ - 1, 1) - knots
    out = []
    for values in (knots, steps):
        line = jnp.broadcast_to(values[channel : channel + 1], (8, LZ))
        if across:
            out.append(line)
            continue
        for first in (0, 8):
            own = jnp.where(iota((8, LZ), 1) == iota((8, LZ), 0) + first, line, 0.0)
            out.append(jnp.broadcast_to(jnp.sum(own, axis=1, keepdims=True), (8, LZ)))
    return out


def interpolate(tables, index, frac):
    halves = []
    for h in (slice(0, 8), slice(8, 16)):
        if len(tables) == 2:
            first, step = gather(tables[0], index[h], 1), gather(tables[1], index[h], 1)
        else:
            row, upper = index[h] & 7, index[h] >= 8
            first = jnp.where(upper, gather(tables[1], row, 0), gather(tables[0], row, 0))
            step = jnp.where(upper, gather(tables[3], row, 0), gather(tables[2], row, 0))
        halves.append(first + frac[h] * step)
    return jnp.concatenate(halves, axis=0)


def depth_kernel(
    inten, memb, syn, transfer, occ,
    weight_x, weight_z, steep, spot, along, tables, own_x, total_x, total_z,
    occ_rows, sigma, prefix, parts,
):
    scale = -2.0 / (LX * 64) / LN2
    dense = knot_table(transfer, 3, scale, False)
    for c in range(3):
        for i, table in enumerate(knot_table(transfer, c, 1.0, c in ACROSS)):
            tables[c, i] = table
    spread = as_bf16(iota((KNOTS, LZ), 1) // 8 == iota((KNOTS, LZ), 0))
    occ_rows[...] = mxu(occ[0].astype(F32).astype(BF16), spread, NN)
    r, k = iota((H, H), 0), iota((H, H), 1)
    diff_y = (jnp.where(k == r + 1, 1.0, 0.0) - jnp.where(k == r - 1, 1.0, 0.0)).astype(BF16)
    k, n = iota((2 * LZ, LZ), 0), iota((2 * LZ, LZ), 1)
    before = as_bf16(k % LZ < n)
    ones = jnp.ones((8, 2 * LZ), BF16)
    for x in range(LX):
        grad_y = mxu(diff_y, inten[x], NN)
        steep[x] = grad_y * grad_y + 1.0
    def cells(j):
        buf = j % 3
        for b in range(0, ROWS, 16):
            rows = pl.ds(j * ROWS + b, 16)
            block = (j * ROWS + b) // 8
            mask = jnp.concatenate(
                [jnp.broadcast_to(occ_rows[block + i : block + i + 1, :], (8, LZ)) for i in range(2)], axis=0
            )
            total = jnp.zeros((16, LZ), F32)
            trans = jnp.ones((16, LZ), F32)
            own_m = jnp.zeros((16, LZ), F32)
            own_s = jnp.zeros((16, LZ), F32)
            for x in range(LX):
                index, frac = lookup(inten[x, rows, :].astype(F32))
                spot[x, rows, :] = index
                along[x, rows, :] = frac
                mem = memb[x, rows, :].astype(F32)
                sy = syn[x, rows, :].astype(F32)
                depth = interpolate(dense, index, frac) + mem * (1.5 * scale)
                depth = (depth + sy * (0.5 * scale)) * mask
                high, low = split(depth)
                row = x * ROWS + b
                parts[buf, 0, row : row + 16, 0:LZ] = high
                parts[buf, 0, row : row + 16, LZ:] = low
                passed = jnp.exp2(depth)
                alpha = 1.0 - passed
                sigma[buf, row : row + 16, :] = alpha
                weight = trans * alpha
                weight_x[x, rows, :] = weight
                own_m = own_m + weight * mem
                own_s = own_s + weight * sy
                trans = trans * passed
                total = total + depth
            total_x[rows, :] = total
            own_x[0, rows, :] = own_m
            own_x[1, rows, :] = own_s
        prefix[buf] = mxu(parts[buf, 0], before, NN)

    def weights(j):
        buf = j % 3
        for x in range(LX):
            for b in range(0, ROWS, 16):
                rows = pl.ds(j * ROWS + b, 16)
                here = slice(x * ROWS + b, x * ROWS + b + 16)
                weight = jnp.exp2(prefix[buf, here, :]) * sigma[buf, here, :]
                weight_z[x, rows, :] = weight
                for i, probability in enumerate((memb, syn)):
                    high, low = split(weight * probability[x, rows, :].astype(F32))
                    parts[buf, 1 + i, here, 0:LZ] = high
                    parts[buf, 1 + i, here, LZ:] = low

    def sums(j):
        buf = j % 3
        deep, own_m, own_s = [mxu(ones, parts[buf, i], NT) for i in range(3)]
        channel = iota((8, LX * ROWS), 0) % 4
        rest = jnp.where(channel == 3, -deep, 0.0)
        for c in range(3):
            rest = jnp.where(channel == c, MEMBRANE_COLOR[c] * own_m + SYNAPSE_COLOR[c] * own_s, rest)
        total_z[j] = rest

    for step in range(H // ROWS + 2):
        if step < H // ROWS:
            cells(step)
        if 1 <= step <= H // ROWS:
            weights(step - 1)
        if step >= 2:
            sums(step - 2)


def shade_kernel(
    pos, inten, weight_x, weight_z, steep, spot, along, tables, own_x, total_x, total_z,
    odd_x, face_a, face_b, even_x,
    keep, send, z_keep, z_send,
    pad, halo, left, dz, parts, zsum, image,
):
    core, zpos = pos[0], pos[1]
    odd_z = zpos % 2
    gx = pos[2]
    low = jnp.where(core == 0, odd_x[...].astype(F32), even_x[...].astype(F32))
    high = jnp.where(core == 0, even_x[...].astype(F32), odd_x[...].astype(F32))
    pad[0] = jnp.where(gx == 0, 0.0, low)
    pad[1] = jnp.where(gx == 63, 0.0, high)
    near = jnp.where(zpos == 0, 0.0, jnp.where(odd_z == 0, face_b[...], face_a[...]))
    far = jnp.where(zpos == 3, 0.0, jnp.where(odd_z == 0, face_a[...], face_b[...]))
    both = jnp.concatenate([near, far], axis=0).astype(BF16)
    halo[...] = mxu(both, as_bf16(iota((16, LZ), 0) == iota((16, LZ), 1)), TN).astype(BF16)
    k, n = iota((2 * LZ, LZ), 0), iota((2 * LZ, LZ), 1)
    up = ((k < LZ) & (k == n + 1)) | ((k >= LZ + LX) & (k < LZ + 2 * LX) & (n == LZ - 1))
    down = ((k < LZ) & (k == n - 1)) | ((k >= LZ) & (k < LZ + LX) & (n == 0))
    diff_z = (jnp.where(up, 1.0, 0.0) - jnp.where(down, 1.0, 0.0)).astype(BF16)
    lanes = iota((ROWS, LZ), 1)
    ones_row = iota((8, 2 * LZ), 0)
    first_half = iota((8, LZ), 0) < 4
    knots = [[tables[c, i] for i in range(2 if c in ACROSS else 4)] for c in range(3)]

    def slopes(j):
        buf, base = j % 2, j * ROWS
        halo_rows = halo[base : base + ROWS, :]
        for x in range(LX):
            mine = jnp.where((lanes == x) | (lanes == LX + x), halo_rows, jnp.zeros_like(halo_rows))
            left[buf, x * ROWS : (x + 1) * ROWS, 0:LZ] = inten[x, base : base + ROWS, :]
            left[buf, x * ROWS : (x + 1) * ROWS, LZ:] = mine
        dz[buf] = mxu(left[buf], diff_z, NN)

    def cells(j, b):
        buf = j % 2
        rows = pl.ds(j * ROWS + b, 16)
        own_m, own_s = own_x[0, rows, :], own_x[1, rows, :]
        acc = [MEMBRANE_COLOR[c] * own_m + SYNAPSE_COLOR[c] * own_s for c in range(3)]
        values = [pad[0, rows, :]] + [inten[x, rows, :].astype(F32) for x in range(LX)] + [pad[1, rows, :]]
        for x in range(LX):
            row = x * ROWS + b
            grad_x = values[x + 2] - values[x]
            grad_z = dz[buf, row : row + 16, :]
            norm = lax.rsqrt(grad_x * grad_x + (grad_z * grad_z + steep[x, rows, :])) * 0.7
            lit_x = (0.3 + jnp.abs(grad_x) * norm) * weight_x[x, rows, :]
            lit_z = (0.3 + jnp.abs(grad_z) * norm) * weight_z[x, rows, :]
            index, frac = spot[x, rows, :], along[x, rows, :]
            for c in range(3):
                color = interpolate(knots[c], index, frac)
                acc[c] = acc[c] + lit_x * color
                high, low = split(lit_z * color)
                parts[buf, c, row : row + 16, 0:LZ] = high
                parts[buf, c, row : row + 16, LZ:] = low
        for c in range(3):
            image[c, rows, :] = acc[c]

    def sums(j, c):
        if c == 0:
            zsum[j] = total_z[j]
        zsum[j] += mxu(as_bf16(ones_row % 4 == c), parts[j % 2, c], NT)

    chunks = H // ROWS
    slopes(0)
    for j in range(chunks):
        for i, b in enumerate(range(0, ROWS, 16)):
            if i == 0 and j + 1 < chunks:
                slopes(j + 1)
            if i < 3 and j > 0:
                sums(j - 1, i)
            cells(j, b)
    for c in range(3):
        sums(chunks - 1, c)
    swap = lambda v: pltpu.roll(v, 4, 0)
    for first in range(0, CHIPS, 8):
        ready = []
        for chip in range(first, first + 8):
            rows = pl.ds(8 * chip, 8)
            a, d, g = [image[c, rows, :] for c in range(3)]
            t = -total_x[rows, :]
            for i, (p, q) in enumerate(((a, d), (g, t))):
                crossed = swap(jnp.where(first_half, q, p))
                for_0 = jnp.where(first_half, p, crossed)
                for_1 = jnp.where(first_half, crossed, q)
                ready.append((keep, chip, i, jnp.where(core == 0, for_0, for_1)))
                ready.append((send, chip, i, jnp.where(core == 0, for_1, for_0)))
        for out, chip, i, value in ready:
            out[chip, 8 * i : 8 * i + 8, :] = value
    for out, chip in ((z_keep, zpos), (z_send, zpos ^ 1)):
        out[...] = jnp.where(iota((8, LX * ROWS), 0) < 4, zsum[chip], zsum[3 - chip])


def depth_rows(b):
    return jnp.where(iota((8, LZ), 0) < 4, pltpu.roll(b, 4, 0), b)


def z_rows(z):
    upper = iota(z.shape, 0) < 4
    return jnp.where(upper, jnp.broadcast_to(z[3:4], z.shape), jnp.broadcast_to(z[7:8], z.shape))


def z_merge(first, second):
    depth_row = iota(first.shape, 0) % 4 == 3
    return first + jnp.where(depth_row, 1.0, jnp.exp2(-z_rows(first))) * second


def z_kernel(pos, z_mine, z_other, z_pair):
    even = pos[1] % 2 == 0
    zm, zo = z_mine[...], z_other[...]
    z_pair[...] = z_merge(jnp.where(even, zm, zo), jnp.where(even, zo, zm))


def pair_kernel(pos, mine, other, code):
    core = pos[0]
    first_half = iota((8, LZ), 0) < 4
    for i in range(CHIPS):
        ma, mb = mine[i, 0:8, :], mine[i, 8:16, :]
        oa, ob = other[i, 0:8, :], other[i, 8:16, :]
        fa, fb = jnp.where(core == 0, ma, oa), jnp.where(core == 0, mb, ob)
        sa, sb = jnp.where(core == 0, oa, ma), jnp.where(core == 0, ob, mb)
        passed = jnp.exp2(-depth_rows(fb))
        a = fa + passed * sa
        b = fb + jnp.where(first_half, passed, 1.0) * sb
        v = jnp.concatenate([a, b], axis=0)
        q = jnp.log2(jnp.maximum(v, 2.0**-25)) * CODE_SCALE + (CODE_MID * CODE_SCALE)
        q = jnp.where(v > 2.0**-25, jnp.round(jnp.minimum(q, 32766.0)), -32768.0)
        code[i] = q.astype(jnp.int32).astype(jnp.int16)


def final_kernel(pos, code, z_mine, z_other, x_image, z_image):
    front = pos[1] < 2
    a = b = deep = jnp.zeros((8, LZ), F32)
    for i in range(CHIPS):
        q = code[i].astype(F32)
        v = jnp.exp2(q * (1.0 / CODE_SCALE) - CODE_MID)
        v = jnp.where(q < -32767.0, 0.0, v)
        passed = jnp.exp2(-deep)
        a = a + passed * v[0:8]
        b = b + passed * v[8:16]
        deep = deep + depth_rows(v[8:16])
    x_image[0] = a[0:4]
    x_image[1] = a[4:8]
    x_image[2] = b[0:4]
    x_image[3] = (1.0 - jnp.exp2(-deep))[0:4]

    zm, zo = z_mine[...], pltpu.roll(z_other[...], 4, 0)
    image = z_merge(jnp.where(front, zm, zo), jnp.where(front, zo, zm))
    image = jnp.where(iota(image.shape, 0) == 3, 1.0 - jnp.exp2(-image), image)
    for x in range(LX):
        z_image[:, x, :] = image[0:4, x * ROWS : (x + 1) * ROWS]


def call(kernel, out_shape, scratch, cost, *operands, wide=False):
    specs = [
        pl.BlockSpec(memory_space=pltpu.SMEM if a.shape == (3,) else pl.ANY if wide else pltpu.VMEM)
        for a in operands
    ]
    return pl.pallas_call(
        kernel,
        out_shape=out_shape,
        in_specs=specs,
        out_specs=[pl.BlockSpec(memory_space=pltpu.VMEM)] * len(out_shape),
        scratch_shapes=scratch,
        compiler_params=pltpu.CompilerParams(vmem_limit_bytes=WIDE if wide else 32 * 2**20),
        cost_estimate=pl.CostEstimate(flops=cost, bytes_accessed=2**20, transcendentals=0),
    )(*operands)


LAYER, FACE = jax.ShapeDtypeStruct((H, LZ), BF16), jax.ShapeDtypeStruct((LX, H), F32)
BRICK = jax.ShapeDtypeStruct((LX, H, LZ), F32)
HALF = jax.ShapeDtypeStruct((CHIPS, 16, LZ), F32)
ZPART = jax.ShapeDtypeStruct((8, LX * ROWS), F32)
IMAGES = [jax.ShapeDtypeStruct((4, 4, LZ), F32), jax.ShapeDtypeStruct((4, LX, ROWS), F32)]
CODE = jax.ShapeDtypeStruct((CHIPS, 16, LZ), jnp.int16)


def faces(*operands):
    brick = jax.ShapeDtypeStruct((LX, H, LZ), BF16)
    outs = [LAYER, FACE, FACE, LAYER, brick, brick, brick]
    return call(faces_kernel, outs, [pltpu.SemaphoreType.DMA((3,))], 10**6, *operands, wide=True)


def depths(intensity, membrane, synapse, transfer, occupancy):
    outs = [BRICK] * 3 + [jax.ShapeDtypeStruct((LX, H, LZ), jnp.int32), BRICK] + [
        jax.ShapeDtypeStruct((3, 4, 8, LZ), F32),
        jax.ShapeDtypeStruct((2, H, LZ), F32),
        jax.ShapeDtypeStruct((H, LZ), F32),
        jax.ShapeDtypeStruct((H // ROWS, 8, LX * ROWS), F32),
    ]
    scratch = [
        pltpu.VMEM((H // 8, LZ), F32),
        pltpu.VMEM((3, LX * ROWS, LZ), F32),
        pltpu.VMEM((3, LX * ROWS, LZ), F32),
        pltpu.VMEM((3, 3, LX * ROWS, 2 * LZ), BF16),
    ]
    return call(depth_kernel, outs, scratch, 10**8, intensity, membrane, synapse, transfer, occupancy)


def shades(*operands):
    scratch = [
        pltpu.VMEM((2, H, LZ), F32),
        pltpu.VMEM((H, LZ), BF16),
        pltpu.VMEM((2, LX * ROWS, 2 * LZ), BF16),
        pltpu.VMEM((2, LX * ROWS, LZ), F32),
        pltpu.VMEM((2, 3, LX * ROWS, 2 * LZ), BF16),
        pltpu.VMEM((H // ROWS, 8, LX * ROWS), F32),
        pltpu.VMEM((3, H, LZ), F32),
    ]
    return call(shade_kernel, [HALF, HALF, ZPART, ZPART], scratch, 10**8, *operands)


def body(intensity, membrane, synapse, transfer, occupancy):
    gx = ("z", "y", "core")
    pos = jnp.stack([lax.axis_index("core"), lax.axis_index("x"), lax.axis_index(gx)]).astype(jnp.int32)
    odd_x, face_a, face_b, even_x, intensity, membrane, synapse = faces(pos, intensity, membrane, synapse)
    even = [p for i in range(0, 64, 2) for p in ((i, i + 1), (i + 1, i))]
    odd = [p for i in range(1, 64, 2) for p in ((i, (i + 1) % 64), ((i + 1) % 64, i))]
    odd_x = lax.ppermute(odd_x, gx, odd)
    face_a = lax.ppermute(face_a, "x", [(0, 1), (1, 0), (2, 3), (3, 2)])
    face_b = lax.ppermute(face_b, "x", [(1, 2), (2, 1), (3, 0), (0, 3)])
    even_x = lax.ppermute(even_x, gx, even)
    transfer = jnp.pad(transfer, ((0, 4), (0, LZ - KNOTS)))
    deep = depths(intensity, membrane, synapse, transfer, occupancy)
    keep, send, z_keep, z_send = shades(
        pos, intensity, *deep, odd_x, face_a, face_b, even_x
    )
    other = lax.ppermute(send, "core", [(0, 1), (1, 0)])
    z_other = lax.ppermute(z_send, "x", [(0, 1), (1, 0), (2, 3), (3, 2)])
    (code,) = call(pair_kernel, [CODE], [], 10**6, pos, keep, other)
    (z_pair,) = call(z_kernel, [ZPART], [], 10**11, pos, z_keep, z_other)
    z_other = lax.ppermute(z_pair, "x", [(0, 3), (3, 0), (1, 2), (2, 1)])
    code = lax.all_to_all(code, ("z", "y"), split_axis=0, concat_axis=0, tiled=True)
    return tuple(call(final_kernel, IMAGES, [], 10**6, pos, code, z_pair, z_other))


def solution(mesh):
    split_mesh = Mesh(mesh.devices.reshape(8, 4, 2, 4), ("z", "y", "core", "x"))
    gx = ("z", "y", "core")
    brick = P(gx, None, "x")
    return jax.shard_map(
        body,
        mesh=split_mesh,
        in_specs=(brick, brick, brick, P(), brick),
        out_specs=(P(None, gx, "x"), P(None, gx, "x")),
        check_vma=False,
    )
```

```python
import jax
import jax.numpy as jnp
from jax import lax
from jax.experimental import pallas as pl
from jax.experimental.pallas import tpu as pltpu
from jax.sharding import Mesh, PartitionSpec as P

MEMBRANE_COLOR = (0.9, 0.2, 0.1)
SYNAPSE_COLOR = (0.1, 0.8, 0.3)
LX, H, LZ = 8, 256, 128
KNOTS = 16
ROWS = 64
CHIPS = 32
ACROSS = ()
WIDE = 52 * 2**20
F32, BF16 = jnp.float32, jnp.bfloat16
CODE_SCALE = 32760.0 / 12.0
CODE_MID = 13.0
LN2 = 0.6931471805599453
NN = (((1,), (0,)), ((), ()))
NT = (((1,), (1,)), ((), ()))
TN = (((0,), (0,)), ((), ()))


def mxu(a, b, dims):
    return lax.dot_general(a, b, dims, preferred_element_type=F32)


def iota(shape, dim):
    return lax.broadcasted_iota(jnp.int32, shape, dim)


def as_bf16(mask, value=1.0):
    return jnp.where(mask, value, 0.0).astype(BF16)


def split(value):
    high = value.astype(BF16)
    return high, (value - high.astype(F32)).astype(BF16)


def faces_kernel(
    pos, inten_hbm, memb_hbm, syn_hbm,
    odd_x, face_a, face_b, even_x, intensity, memb, syn, sems,
):
    pairs = ((inten_hbm, intensity), (memb_hbm, memb), (syn_hbm, syn))
    copies = [pltpu.make_async_copy(a, b, sems.at[i]) for i, (a, b) in enumerate(pairs)]
    for copy in copies:
        copy.start()
    copies[0].wait()
    core, odd_z = pos[0], pos[1] % 2
    even_x[...] = intensity[jnp.where(core == 0, LX - 1, 0)]
    odd_x[...] = intensity[jnp.where(core == 0, 0, LX - 1)]
    row, lane = iota((16, LZ), 0), iota((16, LZ), 1)
    lane_a = jnp.where(odd_z == 0, LZ - 1, 0)
    wanted = jnp.where(row < LX, lane_a, LZ - 1 - lane_a)
    total = jnp.zeros((16, H), F32)
    for x in range(LX):
        pick = as_bf16((row % LX == x) & (lane == wanted))
        total = total + mxu(pick, intensity[x], NT)
    face_a[...] = total[:LX]
    face_b[...] = total[LX:]
    for copy in copies[1:]:
        copy.wait()


def lookup(value):
    t = jnp.clip(value, 0.0, 1.0) * (KNOTS - 1.0)
    index = jnp.minimum(t.astype(jnp.int32), KNOTS - 2)
    return index, t - index.astype(F32)


def gather(table, index, dim):
    numbers = lax.GatherDimensionNumbers(
        offset_dims=(), collapsed_slice_dims=(dim,), start_index_map=(dim,),
        operand_batching_dims=(1 - dim,), start_indices_batching_dims=(1 - dim,),
    )
    return lax.gather(
        table, index[..., None], numbers, (1, 1), mode=lax.GatherScatterMode.PROMISE_IN_BOUNDS
    )


def knot_table(transfer, channel, factor, across):
    knots = transfer[...] * factor
    steps = pltpu.roll(knots, LZ - 1, 1) - knots
    out = []
    for values in (knots, steps):
        line = jnp.broadcast_to(values[channel : channel + 1], (8, LZ))
        if across:
            out.append(line)
            continue
        for first in (0, 8):
            own = jnp.where(iota((8, LZ), 1) == iota((8, LZ), 0) + first, line, 0.0)
            out.append(jnp.broadcast_to(jnp.sum(own, axis=1, keepdims=True), (8, LZ)))
    return out


def interpolate(tables, index, frac):
    halves = []
    for h in (slice(0, 8), slice(8, 16)):
        if len(tables) == 2:
            first, step = gather(tables[0], index[h], 1), gather(tables[1], index[h], 1)
        else:
            row, upper = index[h] & 7, index[h] >= 8
            first = jnp.where(upper, gather(tables[1], row, 0), gather(tables[0], row, 0))
            step = jnp.where(upper, gather(tables[3], row, 0), gather(tables[2], row, 0))
        halves.append(first + frac[h] * step)
    return jnp.concatenate(halves, axis=0)


def depth_kernel(
    inten, memb, syn, transfer, occ,
    weight_x, weight_z, steep, spot, along, tables, own_x, total_x, total_z,
    occ_rows, sigma, prefix, parts, columns,
):
    scale = -2.0 / (LX * 64) / LN2
    dense = knot_table(transfer, 3, scale, False)
    for c in range(3):
        for i, table in enumerate(knot_table(transfer, c, 0.7, c in ACROSS)):
            tables[c, i] = table
    spread = as_bf16(iota((KNOTS, LZ), 1) // 8 == iota((KNOTS, LZ), 0))
    occ_rows[...] = mxu(occ[0].astype(F32).astype(BF16), spread, NN)
    r, k = iota((H, H), 0), iota((H, H), 1)
    diff_y = (jnp.where(k == r + 1, 1.0, 0.0) - jnp.where(k == r - 1, 1.0, 0.0)).astype(BF16)
    k, n = iota((2 * LZ, LZ), 0), iota((2 * LZ, LZ), 1)
    before = as_bf16(k % LZ < n)
    lane = iota((16, LZ), 1)
    for x in range(LX):
        grad_y = mxu(diff_y, inten[x], NN)
        steep[x] = grad_y * grad_y + 1.0
    def cells(j):
        buf = j % 2
        for b in range(0, ROWS, 16):
            rows = pl.ds(j * ROWS + b, 16)
            block = (j * ROWS + b) // 8
            mask = jnp.concatenate(
                [jnp.broadcast_to(occ_rows[block + i : block + i + 1, :], (8, LZ)) for i in range(2)], axis=0
            )
            total = jnp.zeros((16, LZ), F32)
            trans = jnp.ones((16, LZ), F32)
            own_m = jnp.zeros((16, LZ), F32)
            own_s = jnp.zeros((16, LZ), F32)
            column = jnp.zeros((16, LZ), F32)
            for x in range(LX):
                index, frac = lookup(inten[x, rows, :].astype(F32))
                spot[x, rows, :] = index
                along[x, rows, :] = frac
                mem = memb[x, rows, :].astype(F32)
                sy = syn[x, rows, :].astype(F32)
                depth = interpolate(dense, index, frac) + mem * (1.5 * scale)
                depth = (depth + sy * (0.5 * scale)) * mask
                high, low = split(depth)
                row = x * ROWS + b
                parts[buf, row : row + 16, 0:LZ] = high
                parts[buf, row : row + 16, LZ:] = low
                passed = jnp.exp2(depth)
                alpha = 1.0 - passed
                sigma[buf, row : row + 16, :] = alpha
                weight = trans * alpha
                weight_x[x, rows, :] = weight
                own_m = own_m + weight * mem
                own_s = own_s + weight * sy
                trans = trans * passed
                total = total + depth
                column = put(column, 3 * LX + x, depth)
            columns[rows, :] = column
            total_x[rows, :] = total
            own_x[0, rows, :] = own_m
            own_x[1, rows, :] = own_s
        prefix[buf] = mxu(parts[buf], before, NN)

    def weights(j):
        buf = j % 2
        for b in range(0, ROWS, 16):
            rows = pl.ds(j * ROWS + b, 16)
            column = columns[rows, :]
            for x in range(LX):
                here = slice(x * ROWS + b, x * ROWS + b + 16)
                weight = jnp.exp2(prefix[buf, here, :]) * sigma[buf, here, :]
                weight_z[x, rows, :] = weight
                column = put(column, x, weight * memb[x, rows, :].astype(F32))
                column = put(column, LX + x, weight * syn[x, rows, :].astype(F32))
            columns[rows, :] = column

    def put(column, place, value):
        return jnp.where(lane == place, jnp.sum(value, axis=1, keepdims=True), column)

    for step in range(H // ROWS + 1):
        if step < H // ROWS:
            cells(step)
        if step >= 1:
            weights(step - 1)
    for half in range(2):
        lines = jnp.transpose(columns[half * LZ : (half + 1) * LZ, :])
        own_m, own_s, deep = lines[0:LX], lines[LX : 2 * LX], lines[3 * LX : 4 * LX]
        for c in range(3):
            total_z[c * LX : (c + 1) * LX, half * LZ : (half + 1) * LZ] = (
                MEMBRANE_COLOR[c] * own_m + SYNAPSE_COLOR[c] * own_s
            )
        total_z[3 * LX :, half * LZ : (half + 1) * LZ] = -deep


def shade_kernel(
    pos, inten, weight_x, weight_z, steep, spot, along, tables, own_x, total_x, total_z,
    odd_x, face_a, face_b, even_x,
    keep, send, z_keep, z_send,
    pad, halo, left, dz, image, columns,
):
    core, zpos = pos[0], pos[1]
    odd_z = zpos % 2
    gx = pos[2]
    low = jnp.where(core == 0, odd_x[...].astype(F32), even_x[...].astype(F32))
    high = jnp.where(core == 0, even_x[...].astype(F32), odd_x[...].astype(F32))
    pad[0] = jnp.where(gx == 0, 0.0, low)
    pad[1] = jnp.where(gx == 63, 0.0, high)
    near = jnp.where(zpos == 0, 0.0, jnp.where(odd_z == 0, face_b[...], face_a[...]))
    far = jnp.where(zpos == 3, 0.0, jnp.where(odd_z == 0, face_a[...], face_b[...]))
    both = jnp.concatenate([near, far], axis=0).astype(BF16)
    halo[...] = mxu(both, as_bf16(iota((16, LZ), 0) == iota((16, LZ), 1)), TN).astype(BF16)
    k, n = iota((2 * LZ, LZ), 0), iota((2 * LZ, LZ), 1)
    up = ((k < LZ) & (k == n + 1)) | ((k >= LZ + LX) & (k < LZ + 2 * LX) & (n == LZ - 1))
    down = ((k < LZ) & (k == n - 1)) | ((k >= LZ) & (k < LZ + LX) & (n == 0))
    diff_z = (jnp.where(up, 1.0, 0.0) - jnp.where(down, 1.0, 0.0)).astype(BF16)
    lanes = iota((ROWS, LZ), 1)
    lane = iota((16, LZ), 1)
    first_half = iota((8, LZ), 0) < 4
    knots = [[tables[c, i] for i in range(2 if c in ACROSS else 4)] for c in range(3)]

    def slopes(j):
        buf, base = j % 2, j * ROWS
        halo_rows = halo[base : base + ROWS, :]
        for x in range(LX):
            mine = jnp.where((lanes == x) | (lanes == LX + x), halo_rows, jnp.zeros_like(halo_rows))
            left[buf, x * ROWS : (x + 1) * ROWS, 0:LZ] = inten[x, base : base + ROWS, :]
            left[buf, x * ROWS : (x + 1) * ROWS, LZ:] = mine
        dz[buf] = mxu(left[buf], diff_z, NN)

    def cells(j, b):
        buf = j % 2
        rows = pl.ds(j * ROWS + b, 16)
        own_m, own_s = own_x[0, rows, :], own_x[1, rows, :]
        acc = [MEMBRANE_COLOR[c] * own_m + SYNAPSE_COLOR[c] * own_s for c in range(3)]
        column = jnp.zeros((16, LZ), F32)
        values = [pad[0, rows, :]] + [inten[x, rows, :].astype(F32) for x in range(LX)] + [pad[1, rows, :]]
        for x in range(LX):
            row = x * ROWS + b
            grad_x = values[x + 2] - values[x]
            grad_z = dz[buf, row : row + 16, :]
            norm = lax.rsqrt(grad_x * grad_x + (grad_z * grad_z + steep[x, rows, :]))
            lit_x = (0.3 / 0.7 + jnp.abs(grad_x) * norm) * weight_x[x, rows, :]
            lit_z = (0.3 / 0.7 + jnp.abs(grad_z) * norm) * weight_z[x, rows, :]
            index, frac = spot[x, rows, :], along[x, rows, :]
            for c in range(3):
                color = interpolate(knots[c], index, frac)
                acc[c] = acc[c] + lit_x * color
                summed = jnp.sum(lit_z * color, axis=1, keepdims=True)
                column = jnp.where(lane == c * LX + x, summed, column)
        for c in range(3):
            image[c, rows, :] = acc[c]
        columns[rows, :] = column

    chunks = H // ROWS
    slopes(0)
    for j in range(chunks):
        for i, b in enumerate(range(0, ROWS, 16)):
            if i == 0 and j + 1 < chunks:
                slopes(j + 1)
            cells(j, b)
    swap = lambda v: pltpu.roll(v, 4, 0)
    for first in range(0, CHIPS, 8):
        ready = []
        for chip in range(first, first + 8):
            rows = pl.ds(8 * chip, 8)
            a, d, g = [image[c, rows, :] for c in range(3)]
            t = -total_x[rows, :]
            for i, (p, q) in enumerate(((a, d), (g, t))):
                crossed = swap(jnp.where(first_half, q, p))
                for_0 = jnp.where(first_half, p, crossed)
                for_1 = jnp.where(first_half, crossed, q)
                ready.append((keep, chip, i, jnp.where(core == 0, for_0, for_1)))
                ready.append((send, chip, i, jnp.where(core == 0, for_1, for_0)))
        for out, chip, i, value in ready:
            out[chip, 8 * i : 8 * i + 8, :] = value
    low, high = [
        total_z[:, half * LZ : (half + 1) * LZ]
        + jnp.where(
            iota((4 * LX, LZ), 0) < 3 * LX, jnp.transpose(columns[half * LZ : (half + 1) * LZ, :])[: 4 * LX], 0.0
        )
        for half in range(2)
    ]
    near_half = iota((4 * LX, LZ), 1) < ROWS
    outer = jnp.where(near_half, low, high)
    inner = pltpu.roll(jnp.where(near_half, high, low), ROWS, 1)
    edge = (zpos == 0) | (zpos == 3)
    z_keep[...] = jnp.where(edge, outer, inner)
    z_send[...] = jnp.where(edge, inner, outer)


def depth_rows(b):
    return jnp.where(iota((8, LZ), 0) < 4, pltpu.roll(b, 4, 0), b)


def z_merge(first, second):
    passed = jnp.exp2(-first[3 * LX :])
    rows = [first[c * LX : (c + 1) * LX] + passed * second[c * LX : (c + 1) * LX] for c in range(3)]
    return jnp.concatenate(rows + [first[3 * LX :] + second[3 * LX :]], axis=0)


def z_kernel(pos, z_mine, z_other, z_pair):
    even = pos[1] % 2 == 0
    zm, zo = z_mine[...], z_other[...]
    z_pair[...] = z_merge(jnp.where(even, zm, zo), jnp.where(even, zo, zm))


def pair_kernel(pos, mine, other, code):
    core = pos[0]
    first_half = iota((8, LZ), 0) < 4
    for i in range(CHIPS):
        ma, mb = mine[i, 0:8, :], mine[i, 8:16, :]
        oa, ob = other[i, 0:8, :], other[i, 8:16, :]
        fa, fb = jnp.where(core == 0, ma, oa), jnp.where(core == 0, mb, ob)
        sa, sb = jnp.where(core == 0, oa, ma), jnp.where(core == 0, ob, mb)
        passed = jnp.exp2(-depth_rows(fb))
        a = fa + passed * sa
        b = fb + jnp.where(first_half, passed, 1.0) * sb
        v = jnp.concatenate([a, b], axis=0)
        q = jnp.log2(jnp.maximum(v, 2.0**-25)) * CODE_SCALE + (CODE_MID * CODE_SCALE)
        q = jnp.where(v > 2.0**-25, jnp.round(jnp.minimum(q, 32766.0)), -32768.0)
        code[i] = q.astype(jnp.int32).astype(jnp.int16)


def final_kernel(pos, code, z_mine, z_other, x_image, z_image):
    front = pos[1] < 2
    a = b = deep = jnp.zeros((8, LZ), F32)
    for i in range(CHIPS):
        q = code[i].astype(F32)
        v = jnp.exp2(q * (1.0 / CODE_SCALE) - CODE_MID)
        v = jnp.where(q < -32767.0, 0.0, v)
        passed = jnp.exp2(-deep)
        a = a + passed * v[0:8]
        b = b + passed * v[8:16]
        deep = deep + depth_rows(v[8:16])
    x_image[0] = a[0:4]
    x_image[1] = a[4:8]
    x_image[2] = b[0:4]
    x_image[3] = (1.0 - jnp.exp2(-deep))[0:4]

    zm, zo = z_mine[...], z_other[...]
    image = z_merge(jnp.where(front, zm, zo), jnp.where(front, zo, zm))
    image = jnp.where(front, image, pltpu.roll(image, ROWS, 1))[:, 0:ROWS]
    for c in range(3):
        z_image[c] = image[c * LX : (c + 1) * LX]
    z_image[3] = 1.0 - jnp.exp2(-image[3 * LX :])


def call(kernel, out_shape, scratch, cost, *operands, wide=False):
    specs = [
        pl.BlockSpec(memory_space=pltpu.SMEM if a.shape == (3,) else pl.ANY if wide else pltpu.VMEM)
        for a in operands
    ]
    return pl.pallas_call(
        kernel,
        out_shape=out_shape,
        in_specs=specs,
        out_specs=[pl.BlockSpec(memory_space=pltpu.VMEM)] * len(out_shape),
        scratch_shapes=scratch,
        compiler_params=pltpu.CompilerParams(vmem_limit_bytes=WIDE if wide else 32 * 2**20),
        cost_estimate=pl.CostEstimate(flops=cost, bytes_accessed=2**20, transcendentals=0),
    )(*operands)


LAYER, FACE = jax.ShapeDtypeStruct((H, LZ), BF16), jax.ShapeDtypeStruct((LX, H), F32)
BRICK = jax.ShapeDtypeStruct((LX, H, LZ), F32)
HALF = jax.ShapeDtypeStruct((CHIPS, 16, LZ), F32)
ZPART = jax.ShapeDtypeStruct((4 * LX, LZ), F32)
IMAGES = [jax.ShapeDtypeStruct((4, 4, LZ), F32), jax.ShapeDtypeStruct((4, LX, ROWS), F32)]
CODE = jax.ShapeDtypeStruct((CHIPS, 16, LZ), jnp.int16)


def faces(*operands):
    brick = jax.ShapeDtypeStruct((LX, H, LZ), BF16)
    outs = [LAYER, FACE, FACE, LAYER, brick, brick, brick]
    return call(faces_kernel, outs, [pltpu.SemaphoreType.DMA((3,))], 10**6, *operands, wide=True)


def depths(intensity, membrane, synapse, transfer, occupancy):
    outs = [BRICK] * 3 + [jax.ShapeDtypeStruct((LX, H, LZ), jnp.int32), BRICK] + [
        jax.ShapeDtypeStruct((3, 4, 8, LZ), F32),
        jax.ShapeDtypeStruct((2, H, LZ), F32),
        jax.ShapeDtypeStruct((H, LZ), F32),
        jax.ShapeDtypeStruct((4 * LX, H), F32),
    ]
    scratch = [
        pltpu.VMEM((H // 8, LZ), F32),
        pltpu.VMEM((2, LX * ROWS, LZ), F32),
        pltpu.VMEM((2, LX * ROWS, LZ), F32),
        pltpu.VMEM((2, LX * ROWS, 2 * LZ), BF16),
        pltpu.VMEM((H, LZ), F32),
    ]
    return call(depth_kernel, outs, scratch, 10**8, intensity, membrane, synapse, transfer, occupancy)


def shades(*operands):
    scratch = [
        pltpu.VMEM((2, H, LZ), F32),
        pltpu.VMEM((H, LZ), BF16),
        pltpu.VMEM((2, LX * ROWS, 2 * LZ), BF16),
        pltpu.VMEM((2, LX * ROWS, LZ), F32),
        pltpu.VMEM((3, H, LZ), F32),
        pltpu.VMEM((H, LZ), F32),
    ]
    return call(shade_kernel, [HALF, HALF, ZPART, ZPART], scratch, 10**8, *operands)


def body(intensity, membrane, synapse, transfer, occupancy):
    gx = ("z", "y", "core")
    pos = jnp.stack([lax.axis_index("core"), lax.axis_index("x"), lax.axis_index(gx)]).astype(jnp.int32)
    odd_x, face_a, face_b, even_x, intensity, membrane, synapse = faces(pos, intensity, membrane, synapse)
    even = [p for i in range(0, 64, 2) for p in ((i, i + 1), (i + 1, i))]
    odd = [p for i in range(1, 64, 2) for p in ((i, (i + 1) % 64), ((i + 1) % 64, i))]
    odd_x = lax.ppermute(odd_x, gx, odd)
    face_a = lax.ppermute(face_a, "x", [(0, 1), (1, 0), (2, 3), (3, 2)])
    face_b = lax.ppermute(face_b, "x", [(1, 2), (2, 1), (3, 0), (0, 3)])
    even_x = lax.ppermute(even_x, gx, even)
    transfer = jnp.pad(transfer, ((0, 4), (0, LZ - KNOTS)))
    deep = depths(intensity, membrane, synapse, transfer, occupancy)
    keep, send, z_keep, z_send = shades(
        pos, intensity, *deep, odd_x, face_a, face_b, even_x
    )
    other = lax.ppermute(send, "core", [(0, 1), (1, 0)])
    z_other = lax.ppermute(z_send, "x", [(0, 1), (1, 0), (2, 3), (3, 2)])
    (code,) = call(pair_kernel, [CODE], [], 10**6, pos, keep, other)
    (z_pair,) = call(z_kernel, [ZPART], [], 10**11, pos, z_keep, z_other)
    z_other = lax.ppermute(z_pair, "x", [(0, 3), (3, 0), (1, 2), (2, 1)])
    code = lax.all_to_all(code, ("z", "y"), split_axis=0, concat_axis=0, tiled=True)
    return tuple(call(final_kernel, IMAGES, [], 10**6, pos, code, z_pair, z_other))


def solution(mesh):
    split_mesh = Mesh(mesh.devices.reshape(8, 4, 2, 4), ("z", "y", "core", "x"))
    gx = ("z", "y", "core")
    brick = P(gx, None, "x")
    return jax.shard_map(
        body,
        mesh=split_mesh,
        in_specs=(brick, brick, brick, P(), brick),
        out_specs=(P(None, gx, "x"), P(None, gx, "x")),
        check_vma=False,
    )
```

```python
import jax
import jax.numpy as jnp
from jax import lax
from jax.experimental import pallas as pl
from jax.experimental.pallas import tpu as pltpu
from jax.sharding import Mesh, PartitionSpec as P

MEMBRANE_COLOR = (0.9, 0.2, 0.1)
SYNAPSE_COLOR = (0.1, 0.8, 0.3)
LX, H, LZ = 8, 256, 128
KNOTS = 16
ROWS = 64
CHIPS = 32
ACROSS = ()
WIDE = 52 * 2**20
F32, BF16 = jnp.float32, jnp.bfloat16
CODE_SCALE = 32760.0 / 12.0
CODE_MID = 13.0
LN2 = 0.6931471805599453
NN = (((1,), (0,)), ((), ()))
NT = (((1,), (1,)), ((), ()))
TN = (((0,), (0,)), ((), ()))


def mxu(a, b, dims):
    return lax.dot_general(a, b, dims, preferred_element_type=F32)


def iota(shape, dim):
    return lax.broadcasted_iota(jnp.int32, shape, dim)


def as_bf16(mask, value=1.0):
    return jnp.where(mask, value, 0.0).astype(BF16)


def split(value):
    high = value.astype(BF16)
    return high, (value - high.astype(F32)).astype(BF16)


def faces_kernel(
    marks, inten_hbm, memb_hbm, syn_hbm,
    odd_x, face_a, face_b, even_x, intensity, memb, syn, sems,
):
    pairs = ((inten_hbm, intensity), (memb_hbm, memb), (syn_hbm, syn))
    copies = [pltpu.make_async_copy(a, b, sems.at[i]) for i, (a, b) in enumerate(pairs)]
    for copy in copies:
        copy.start()
    copies[0].wait()
    core, odd_z = marks[0:1, :], marks[1:2, :] & 1
    first, last = intensity[0].astype(F32), intensity[LX - 1].astype(F32)
    even_x[...] = jnp.where(core == 0, last, first).astype(BF16)
    odd_x[...] = jnp.where(core == 0, first, last).astype(BF16)
    row, lane = iota((16, LZ), 0), iota((16, LZ), 1)
    lane_a = jnp.where(odd_z == 0, LZ - 1, 0)
    wanted = jnp.where(row < LX, lane_a, LZ - 1 - lane_a)
    total = jnp.zeros((16, H), F32)
    for x in range(LX):
        pick = as_bf16((row % LX == x) & (lane == wanted))
        total = total + mxu(pick, intensity[x], NT)
    face_a[...] = total[:LX]
    face_b[...] = total[LX:]
    for copy in copies[1:]:
        copy.wait()


def lookup(value):
    t = jnp.clip(value, 0.0, 1.0) * (KNOTS - 1.0)
    index = jnp.minimum(t.astype(jnp.int32), KNOTS - 2)
    return index, t - index.astype(F32)


def gather(table, index, dim):
    numbers = lax.GatherDimensionNumbers(
        offset_dims=(), collapsed_slice_dims=(dim,), start_index_map=(dim,),
        operand_batching_dims=(1 - dim,), start_indices_batching_dims=(1 - dim,),
    )
    return lax.gather(
        table, index[..., None], numbers, (1, 1), mode=lax.GatherScatterMode.PROMISE_IN_BOUNDS
    )


def knot_table(transfer, channel, factor, across):
    knots = transfer[...] * factor
    steps = pltpu.roll(knots, LZ - 1, 1) - knots
    out = []
    for values in (knots, steps):
        line = jnp.broadcast_to(values[channel : channel + 1], (8, LZ))
        if across:
            out.append(line)
            continue
        for first in (0, 8):
            own = jnp.where(iota((8, LZ), 1) == iota((8, LZ), 0) + first, line, 0.0)
            out.append(jnp.broadcast_to(jnp.sum(own, axis=1, keepdims=True), (8, LZ)))
    return out


def interpolate(tables, index, frac):
    halves = []
    for h in (slice(0, 8), slice(8, 16)):
        if len(tables) == 2:
            first, step = gather(tables[0], index[h], 1), gather(tables[1], index[h], 1)
        else:
            row, upper = index[h] & 7, index[h] >= 8
            first = jnp.where(upper, gather(tables[1], row, 0), gather(tables[0], row, 0))
            step = jnp.where(upper, gather(tables[3], row, 0), gather(tables[2], row, 0))
        halves.append(first + frac[h] * step)
    return jnp.concatenate(halves, axis=0)


def depth_kernel(
    inten, memb, syn, transfer, occ,
    weight_x, weight_z, steep, spot, along, tables, own_x, total_x, total_z,
    occ_rows, sigma, prefix, parts, columns,
):
    scale = -2.0 / (LX * 64) / LN2
    dense = knot_table(transfer, 3, scale, False)
    for c in range(3):
        for i, table in enumerate(knot_table(transfer, c, 0.7, c in ACROSS)):
            tables[c, i] = table
    spread = as_bf16(iota((KNOTS, LZ), 1) // 8 == iota((KNOTS, LZ), 0))
    occ_rows[...] = mxu(occ[0].astype(F32).astype(BF16), spread, NN)
    r, k = iota((H, H), 0), iota((H, H), 1)
    diff_y = (jnp.where(k == r + 1, 1.0, 0.0) - jnp.where(k == r - 1, 1.0, 0.0)).astype(BF16)
    k, n = iota((2 * LZ, LZ), 0), iota((2 * LZ, LZ), 1)
    before = as_bf16(k % LZ < n)
    lane = iota((16, LZ), 1)
    for x in range(LX):
        grad_y = mxu(diff_y, inten[x], NN)
        steep[x] = grad_y * grad_y + 1.0
    def cells(j):
        buf = j % 2
        for b in range(0, ROWS, 16):
            rows = pl.ds(j * ROWS + b, 16)
            block = (j * ROWS + b) // 8
            mask = jnp.concatenate(
                [jnp.broadcast_to(occ_rows[block + i : block + i + 1, :], (8, LZ)) for i in range(2)], axis=0
            )
            total = jnp.zeros((16, LZ), F32)
            trans = jnp.ones((16, LZ), F32)
            own_m = jnp.zeros((16, LZ), F32)
            own_s = jnp.zeros((16, LZ), F32)
            column = jnp.zeros((16, LZ), F32)
            for x in range(LX):
                index, frac = lookup(inten[x, rows, :].astype(F32))
                spot[x, rows, :] = index
                along[x, rows, :] = frac
                mem = memb[x, rows, :].astype(F32)
                sy = syn[x, rows, :].astype(F32)
                depth = interpolate(dense, index, frac) + mem * (1.5 * scale)
                depth = (depth + sy * (0.5 * scale)) * mask
                high, low = split(depth)
                row = x * ROWS + b
                parts[buf, row : row + 16, 0:LZ] = high
                parts[buf, row : row + 16, LZ:] = low
                passed = jnp.exp2(depth)
                alpha = 1.0 - passed
                sigma[buf, row : row + 16, :] = alpha
                weight = trans * alpha
                weight_x[x, rows, :] = weight
                own_m = own_m + weight * mem
                own_s = own_s + weight * sy
                trans = trans * passed
                total = total + depth
                column = put(column, 3 * LX + x, depth)
            columns[rows, :] = column
            total_x[rows, :] = total
            own_x[0, rows, :] = own_m
            own_x[1, rows, :] = own_s
        prefix[buf] = mxu(parts[buf], before, NN)

    def weights(j):
        buf = j % 2
        for b in range(0, ROWS, 16):
            rows = pl.ds(j * ROWS + b, 16)
            column = columns[rows, :]
            for x in range(LX):
                here = slice(x * ROWS + b, x * ROWS + b + 16)
                weight = jnp.exp2(prefix[buf, here, :]) * sigma[buf, here, :]
                weight_z[x, rows, :] = weight
                column = put(column, x, weight * memb[x, rows, :].astype(F32))
                column = put(column, LX + x, weight * syn[x, rows, :].astype(F32))
            columns[rows, :] = column

    def put(column, place, value):
        return jnp.where(lane == place, jnp.sum(value, axis=1, keepdims=True), column)

    for step in range(H // ROWS + 1):
        if step < H // ROWS:
            cells(step)
        if step >= 1:
            weights(step - 1)
    for half in range(2):
        lines = jnp.transpose(columns[half * LZ : (half + 1) * LZ, :])
        own_m, own_s, deep = lines[0:LX], lines[LX : 2 * LX], lines[3 * LX : 4 * LX]
        for c in range(3):
            total_z[c * LX : (c + 1) * LX, half * LZ : (half + 1) * LZ] = (
                MEMBRANE_COLOR[c] * own_m + SYNAPSE_COLOR[c] * own_s
            )
        total_z[3 * LX :, half * LZ : (half + 1) * LZ] = -deep


def shade_kernel(
    marks, inten, weight_x, weight_z, steep, spot, along, tables, own_x, total_x, total_z,
    odd_x, face_a, face_b, even_x,
    keep, send, z_keep, z_send,
    pad, halo, left, dz, image, columns,
):
    core, zpos, gx = marks[0:1, :], marks[1:2, :], marks[2:3, :]
    lane_z = jnp.concatenate([zpos, zpos], axis=1)
    odd_z = lane_z & 1
    low = jnp.where(core == 0, odd_x[...].astype(F32), even_x[...].astype(F32))
    high = jnp.where(core == 0, even_x[...].astype(F32), odd_x[...].astype(F32))
    pad[0] = jnp.where(gx == 0, 0.0, low)
    pad[1] = jnp.where(gx == 63, 0.0, high)
    near = jnp.where(lane_z == 0, 0.0, jnp.where(odd_z == 0, face_b[...], face_a[...]))
    far = jnp.where(lane_z == 3, 0.0, jnp.where(odd_z == 0, face_a[...], face_b[...]))
    both = jnp.concatenate([near, far], axis=0).astype(BF16)
    halo[...] = mxu(both, as_bf16(iota((16, LZ), 0) == iota((16, LZ), 1)), TN).astype(BF16)
    k, n = iota((2 * LZ, LZ), 0), iota((2 * LZ, LZ), 1)
    up = ((k < LZ) & (k == n + 1)) | ((k >= LZ + LX) & (k < LZ + 2 * LX) & (n == LZ - 1))
    down = ((k < LZ) & (k == n - 1)) | ((k >= LZ) & (k < LZ + LX) & (n == 0))
    diff_z = (jnp.where(up, 1.0, 0.0) - jnp.where(down, 1.0, 0.0)).astype(BF16)
    lanes = iota((ROWS, LZ), 1)
    lane = iota((16, LZ), 1)
    first_half = iota((8, LZ), 0) < 4
    knots = [[tables[c, i] for i in range(2 if c in ACROSS else 4)] for c in range(3)]

    def slopes(j):
        buf, base = j % 2, j * ROWS
        halo_rows = halo[base : base + ROWS, :]
        for x in range(LX):
            mine = jnp.where((lanes == x) | (lanes == LX + x), halo_rows, jnp.zeros_like(halo_rows))
            left[buf, x * ROWS : (x + 1) * ROWS, 0:LZ] = inten[x, base : base + ROWS, :]
            left[buf, x * ROWS : (x + 1) * ROWS, LZ:] = mine
        dz[buf] = mxu(left[buf], diff_z, NN)

    def cells(j, b):
        buf = j % 2
        rows = pl.ds(j * ROWS + b, 16)
        own_m, own_s = own_x[0, rows, :], own_x[1, rows, :]
        acc = [MEMBRANE_COLOR[c] * own_m + SYNAPSE_COLOR[c] * own_s for c in range(3)]
        column = jnp.zeros((16, LZ), F32)
        values = [pad[0, rows, :]] + [inten[x, rows, :].astype(F32) for x in range(LX)] + [pad[1, rows, :]]
        for x in range(LX):
            row = x * ROWS + b
            grad_x = values[x + 2] - values[x]
            grad_z = dz[buf, row : row + 16, :]
            norm = lax.rsqrt(grad_x * grad_x + (grad_z * grad_z + steep[x, rows, :]))
            lit_x = (0.3 / 0.7 + jnp.abs(grad_x) * norm) * weight_x[x, rows, :]
            lit_z = (0.3 / 0.7 + jnp.abs(grad_z) * norm) * weight_z[x, rows, :]
            index, frac = spot[x, rows, :], along[x, rows, :]
            for c in range(3):
                color = interpolate(knots[c], index, frac)
                acc[c] = acc[c] + lit_x * color
                summed = jnp.sum(lit_z * color, axis=1, keepdims=True)
                column = jnp.where(lane == c * LX + x, summed, column)
        for c in range(3):
            image[c, rows, :] = acc[c]
        columns[rows, :] = column

    chunks = H // ROWS
    slopes(0)
    for j in range(chunks):
        for i, b in enumerate(range(0, ROWS, 16)):
            if i == 0 and j + 1 < chunks:
                slopes(j + 1)
            cells(j, b)
    swap = lambda v: pltpu.roll(v, 4, 0)
    for first in range(0, CHIPS, 8):
        ready = []
        for chip in range(first, first + 8):
            rows = pl.ds(8 * chip, 8)
            a, d, g = [image[c, rows, :] for c in range(3)]
            t = -total_x[rows, :]
            for i, (p, q) in enumerate(((a, d), (g, t))):
                crossed = swap(jnp.where(first_half, q, p))
                for_0 = jnp.where(first_half, p, crossed)
                for_1 = jnp.where(first_half, crossed, q)
                ready.append((keep, chip, i, jnp.where(core == 0, for_0, for_1)))
                ready.append((send, chip, i, jnp.where(core == 0, for_1, for_0)))
        for out, chip, i, value in ready:
            out[chip, 8 * i : 8 * i + 8, :] = value
    low, high = [
        total_z[:, half * LZ : (half + 1) * LZ]
        + jnp.where(
            iota((4 * LX, LZ), 0) < 3 * LX, jnp.transpose(columns[half * LZ : (half + 1) * LZ, :])[: 4 * LX], 0.0
        )
        for half in range(2)
    ]
    near_half = iota((4 * LX, LZ), 1) < ROWS
    outer = jnp.where(near_half, low, high)
    inner = pltpu.roll(jnp.where(near_half, high, low), ROWS, 1)
    edge = (zpos == 0) | (zpos == 3)
    z_keep[...] = jnp.where(edge, outer, inner)
    z_send[...] = jnp.where(edge, inner, outer)


def depth_rows(b):
    return jnp.where(iota((8, LZ), 0) < 4, pltpu.roll(b, 4, 0), b)


def z_merge(first, second):
    passed = jnp.exp2(-first[3 * LX :])
    rows = [first[c * LX : (c + 1) * LX] + passed * second[c * LX : (c + 1) * LX] for c in range(3)]
    return jnp.concatenate(rows + [first[3 * LX :] + second[3 * LX :]], axis=0)


def z_kernel(marks, z_mine, z_other, z_pair):
    even = (marks[1:2, :] & 1) == 0
    zm, zo = z_mine[...], z_other[...]
    z_pair[...] = z_merge(jnp.where(even, zm, zo), jnp.where(even, zo, zm))


def pair_kernel(marks, mine, other, code):
    core = marks[0:1, :]
    first_half = iota((8, LZ), 0) < 4
    for i in range(CHIPS):
        ma, mb = mine[i, 0:8, :], mine[i, 8:16, :]
        oa, ob = other[i, 0:8, :], other[i, 8:16, :]
        fa, fb = jnp.where(core == 0, ma, oa), jnp.where(core == 0, mb, ob)
        sa, sb = jnp.where(core == 0, oa, ma), jnp.where(core == 0, ob, mb)
        passed = jnp.exp2(-depth_rows(fb))
        a = fa + passed * sa
        b = fb + jnp.where(first_half, passed, 1.0) * sb
        v = jnp.concatenate([a, b], axis=0)
        q = jnp.log2(jnp.maximum(v, 2.0**-25)) * CODE_SCALE + (CODE_MID * CODE_SCALE)
        q = jnp.where(v > 2.0**-25, jnp.round(jnp.minimum(q, 32766.0)), -32768.0)
        code[i] = q.astype(jnp.int32).astype(jnp.int16)


def final_kernel(marks, code, z_mine, z_other, x_image, z_image):
    front = marks[1:2, :] < 2
    a = b = deep = jnp.zeros((8, LZ), F32)
    for i in range(CHIPS):
        q = code[i].astype(F32)
        v = jnp.exp2(q * (1.0 / CODE_SCALE) - CODE_MID)
        v = jnp.where(q < -32767.0, 0.0, v)
        passed = jnp.exp2(-deep)
        a = a + passed * v[0:8]
        b = b + passed * v[8:16]
        deep = deep + depth_rows(v[8:16])
    x_image[0] = a[0:4]
    x_image[1] = a[4:8]
    x_image[2] = b[0:4]
    x_image[3] = (1.0 - jnp.exp2(-deep))[0:4]

    zm, zo = z_mine[...], z_other[...]
    image = z_merge(jnp.where(front, zm, zo), jnp.where(front, zo, zm))
    image = jnp.where(front, image, pltpu.roll(image, ROWS, 1))[:, 0:ROWS]
    for c in range(3):
        z_image[c] = image[c * LX : (c + 1) * LX]
    z_image[3] = 1.0 - jnp.exp2(-image[3 * LX :])


def call(kernel, out_shape, scratch, cost, *operands, wide=False):
    specs = [
        pl.BlockSpec(memory_space=pl.ANY if wide and a.ndim == 3 else pltpu.VMEM)
        for a in operands
    ]
    return pl.pallas_call(
        kernel,
        out_shape=out_shape,
        in_specs=specs,
        out_specs=[pl.BlockSpec(memory_space=pltpu.VMEM)] * len(out_shape),
        scratch_shapes=scratch,
        compiler_params=pltpu.CompilerParams(vmem_limit_bytes=WIDE if wide else 32 * 2**20),
        cost_estimate=pl.CostEstimate(flops=cost, bytes_accessed=2**20, transcendentals=0),
    )(*operands)


LAYER, FACE = jax.ShapeDtypeStruct((H, LZ), BF16), jax.ShapeDtypeStruct((LX, H), F32)
BRICK = jax.ShapeDtypeStruct((LX, H, LZ), F32)
HALF = jax.ShapeDtypeStruct((CHIPS, 16, LZ), F32)
ZPART = jax.ShapeDtypeStruct((4 * LX, LZ), F32)
IMAGES = [jax.ShapeDtypeStruct((4, 4, LZ), F32), jax.ShapeDtypeStruct((4, LX, ROWS), F32)]
CODE = jax.ShapeDtypeStruct((CHIPS, 16, LZ), jnp.int16)


def faces(*operands):
    brick = jax.ShapeDtypeStruct((LX, H, LZ), BF16)
    outs = [LAYER, FACE, FACE, LAYER, brick, brick, brick]
    return call(faces_kernel, outs, [pltpu.SemaphoreType.DMA((3,))], 10**6, *operands, wide=True)


def depths(intensity, membrane, synapse, transfer, occupancy):
    outs = [BRICK] * 3 + [jax.ShapeDtypeStruct((LX, H, LZ), jnp.int32), BRICK] + [
        jax.ShapeDtypeStruct((3, 4, 8, LZ), F32),
        jax.ShapeDtypeStruct((2, H, LZ), F32),
        jax.ShapeDtypeStruct((H, LZ), F32),
        jax.ShapeDtypeStruct((4 * LX, H), F32),
    ]
    scratch = [
        pltpu.VMEM((H // 8, LZ), F32),
        pltpu.VMEM((2, LX * ROWS, LZ), F32),
        pltpu.VMEM((2, LX * ROWS, LZ), F32),
        pltpu.VMEM((2, LX * ROWS, 2 * LZ), BF16),
        pltpu.VMEM((H, LZ), F32),
    ]
    return call(depth_kernel, outs, scratch, 10**8, intensity, membrane, synapse, transfer, occupancy)


def shades(*operands):
    scratch = [
        pltpu.VMEM((2, H, LZ), F32),
        pltpu.VMEM((H, LZ), BF16),
        pltpu.VMEM((2, LX * ROWS, 2 * LZ), BF16),
        pltpu.VMEM((2, LX * ROWS, LZ), F32),
        pltpu.VMEM((3, H, LZ), F32),
        pltpu.VMEM((H, LZ), F32),
    ]
    return call(shade_kernel, [HALF, HALF, ZPART, ZPART], scratch, 10**8, *operands)


def body(intensity, membrane, synapse, transfer, occupancy):
    gx = ("z", "y", "core")
    place = jnp.stack([lax.axis_index("core"), lax.axis_index("x"), lax.axis_index(gx)]).astype(jnp.int32)
    marks = jnp.broadcast_to(jnp.pad(place, (0, 5))[:, None], (8, LZ))
    odd_x, face_a, face_b, even_x, intensity, membrane, synapse = faces(marks, intensity, membrane, synapse)
    even = [p for i in range(0, 64, 2) for p in ((i, i + 1), (i + 1, i))]
    odd = [p for i in range(1, 64, 2) for p in ((i, (i + 1) % 64), ((i + 1) % 64, i))]
    odd_x = lax.ppermute(odd_x, gx, odd)
    face_a = lax.ppermute(face_a, "x", [(0, 1), (1, 0), (2, 3), (3, 2)])
    face_b = lax.ppermute(face_b, "x", [(1, 2), (2, 1), (3, 0), (0, 3)])
    even_x = lax.ppermute(even_x, gx, even)
    transfer = jnp.pad(transfer, ((0, 4), (0, LZ - KNOTS)))
    deep = depths(intensity, membrane, synapse, transfer, occupancy)
    keep, send, z_keep, z_send = shades(
        marks, intensity, *deep, odd_x, face_a, face_b, even_x
    )
    other = lax.ppermute(send, "core", [(0, 1), (1, 0)])
    z_other = lax.ppermute(z_send, "x", [(0, 1), (1, 0), (2, 3), (3, 2)])
    (code,) = call(pair_kernel, [CODE], [], 10**6, marks, keep, other)
    (z_pair,) = call(z_kernel, [ZPART], [], 10**11, marks, z_keep, z_other)
    z_other = lax.ppermute(z_pair, "x", [(0, 3), (3, 0), (1, 2), (2, 1)])
    code = lax.all_to_all(code, ("z", "y"), split_axis=0, concat_axis=0, tiled=True)
    return tuple(call(final_kernel, IMAGES, [], 10**6, marks, code, z_pair, z_other))


def solution(mesh):
    split_mesh = Mesh(mesh.devices.reshape(8, 4, 2, 4), ("z", "y", "core", "x"))
    gx = ("z", "y", "core")
    brick = P(gx, None, "x")
    return jax.shard_map(
        body,
        mesh=split_mesh,
        in_specs=(brick, brick, brick, P(), brick),
        out_specs=(P(None, gx, "x"), P(None, gx, "x")),
        check_vma=False,
    )
```

```python
import jax
import jax.numpy as jnp
from jax import lax
from jax.experimental import pallas as pl
from jax.experimental.pallas import tpu as pltpu
from jax.sharding import Mesh, PartitionSpec as P

MEMBRANE_COLOR = (0.9, 0.2, 0.1)
SYNAPSE_COLOR = (0.1, 0.8, 0.3)
LX, H, LZ = 8, 256, 128
KNOTS = 16
ROWS = 64
CHIPS = 32
EARLY = 1
ACROSS = ()
WIDE = 52 * 2**20
F32, BF16 = jnp.float32, jnp.bfloat16
CODE_SCALE = 32760.0 / 12.0
CODE_MID = 13.0
LN2 = 0.6931471805599453
NN = (((1,), (0,)), ((), ()))
NT = (((1,), (1,)), ((), ()))
TN = (((0,), (0,)), ((), ()))


def mxu(a, b, dims):
    return lax.dot_general(a, b, dims, preferred_element_type=F32)


def iota(shape, dim):
    return lax.broadcasted_iota(jnp.int32, shape, dim)


def as_bf16(mask, value=1.0):
    return jnp.where(mask, value, 0.0).astype(BF16)


def split(value):
    high = value.astype(BF16)
    return high, (value - high.astype(F32)).astype(BF16)


def faces_kernel(
    marks, inten_hbm, memb_hbm, syn_hbm,
    odd_x, face_a, face_b, even_x, intensity, memb, syn, sems,
):
    pairs = ((inten_hbm, intensity), (memb_hbm, memb), (syn_hbm, syn))
    copies = [pltpu.make_async_copy(a, b, sems.at[i]) for i, (a, b) in enumerate(pairs)]
    for copy in copies:
        copy.start()
    copies[0].wait()
    core, odd_z = marks[0:1, :], marks[1:2, :] & 1
    first, last = intensity[0].astype(F32), intensity[LX - 1].astype(F32)
    even_x[...] = jnp.where(core == 0, last, first).astype(BF16)
    odd_x[...] = jnp.where(core == 0, first, last).astype(BF16)
    row, lane = iota((16, LZ), 0), iota((16, LZ), 1)
    lane_a = jnp.where(odd_z == 0, LZ - 1, 0)
    wanted = jnp.where(row < LX, lane_a, LZ - 1 - lane_a)
    total = jnp.zeros((16, H), F32)
    for x in range(LX):
        pick = as_bf16((row % LX == x) & (lane == wanted))
        total = total + mxu(pick, intensity[x], NT)
    face_a[...] = total[:LX]
    face_b[...] = total[LX:]
    for copy in copies[1:]:
        copy.wait()


def lookup(value):
    t = jnp.clip(value, 0.0, 1.0) * (KNOTS - 1.0)
    index = jnp.minimum(t.astype(jnp.int32), KNOTS - 2)
    return index, t - index.astype(F32)


def gather(table, index, dim):
    numbers = lax.GatherDimensionNumbers(
        offset_dims=(), collapsed_slice_dims=(dim,), start_index_map=(dim,),
        operand_batching_dims=(1 - dim,), start_indices_batching_dims=(1 - dim,),
    )
    return lax.gather(
        table, index[..., None], numbers, (1, 1), mode=lax.GatherScatterMode.PROMISE_IN_BOUNDS
    )


def knot_table(transfer, channel, factor, across):
    knots = transfer[...] * factor
    steps = pltpu.roll(knots, LZ - 1, 1) - knots
    out = []
    for values in (knots, steps):
        line = jnp.broadcast_to(values[channel : channel + 1], (8, LZ))
        if across:
            out.append(line)
            continue
        for first in (0, 8):
            own = jnp.where(iota((8, LZ), 1) == iota((8, LZ), 0) + first, line, 0.0)
            out.append(jnp.broadcast_to(jnp.sum(own, axis=1, keepdims=True), (8, LZ)))
    return out


def interpolate(tables, index, frac):
    halves = []
    for h in (slice(0, 8), slice(8, 16)):
        if len(tables) == 2:
            first, step = gather(tables[0], index[h], 1), gather(tables[1], index[h], 1)
        else:
            row, upper = index[h] & 7, index[h] >= 8
            first = jnp.where(upper, gather(tables[1], row, 0), gather(tables[0], row, 0))
            step = jnp.where(upper, gather(tables[3], row, 0), gather(tables[2], row, 0))
        halves.append(first + frac[h] * step)
    return jnp.concatenate(halves, axis=0)


def depth_kernel(
    inten, memb, syn, transfer, occ,
    weight_x, weight_z, steep, hue, spot, along, tables, own_x, total_x, total_z,
    occ_rows, sigma, prefix, parts, columns,
):
    scale = -2.0 / (LX * 64) / LN2
    dense = knot_table(transfer, 3, scale, False)
    knots = [knot_table(transfer, c, 0.7, c in ACROSS) for c in range(3)]
    for c in range(EARLY, 3):
        for i, table in enumerate(knots[c]):
            tables[c - EARLY, i] = table
    spread = as_bf16(iota((KNOTS, LZ), 1) // 8 == iota((KNOTS, LZ), 0))
    occ_rows[...] = mxu(occ[0].astype(F32).astype(BF16), spread, NN)
    r, k = iota((H, H), 0), iota((H, H), 1)
    diff_y = (jnp.where(k == r + 1, 1.0, 0.0) - jnp.where(k == r - 1, 1.0, 0.0)).astype(BF16)
    k, n = iota((2 * LZ, LZ), 0), iota((2 * LZ, LZ), 1)
    before = as_bf16(k % LZ < n)
    lane = iota((16, LZ), 1)
    for x in range(LX):
        grad_y = mxu(diff_y, inten[x], NN)
        steep[x] = grad_y * grad_y + 1.0
    def cells(j):
        buf = j % 2
        for b in range(0, ROWS, 16):
            rows = pl.ds(j * ROWS + b, 16)
            block = (j * ROWS + b) // 8
            mask = jnp.concatenate(
                [jnp.broadcast_to(occ_rows[block + i : block + i + 1, :], (8, LZ)) for i in range(2)], axis=0
            )
            total = jnp.zeros((16, LZ), F32)
            trans = jnp.ones((16, LZ), F32)
            own_m = jnp.zeros((16, LZ), F32)
            own_s = jnp.zeros((16, LZ), F32)
            column = jnp.zeros((16, LZ), F32)
            for x in range(LX):
                index, frac = lookup(inten[x, rows, :].astype(F32))
                spot[x, rows, :] = index
                along[x, rows, :] = frac
                for c in range(EARLY):
                    hue[c, x, rows, :] = interpolate(knots[c], index, frac)
                mem = memb[x, rows, :].astype(F32)
                sy = syn[x, rows, :].astype(F32)
                depth = interpolate(dense, index, frac) + mem * (1.5 * scale)
                depth = (depth + sy * (0.5 * scale)) * mask
                high, low = split(depth)
                row = x * ROWS + b
                parts[buf, row : row + 16, 0:LZ] = high
                parts[buf, row : row + 16, LZ:] = low
                passed = jnp.exp2(depth)
                alpha = 1.0 - passed
                sigma[buf, row : row + 16, :] = alpha
                weight = trans * alpha
                weight_x[x, rows, :] = weight
                own_m = own_m + weight * mem
                own_s = own_s + weight * sy
                trans = trans * passed
                total = total + depth
                column = put(column, 3 * LX + x, depth)
            columns[rows, :] = column
            total_x[rows, :] = total
            own_x[0, rows, :] = own_m
            own_x[1, rows, :] = own_s
        prefix[buf] = mxu(parts[buf], before, NN)

    def weights(j):
        buf = j % 2
        for b in range(0, ROWS, 16):
            rows = pl.ds(j * ROWS + b, 16)
            column = columns[rows, :]
            for x in range(LX):
                here = slice(x * ROWS + b, x * ROWS + b + 16)
                weight = jnp.exp2(prefix[buf, here, :]) * sigma[buf, here, :]
                weight_z[x, rows, :] = weight
                column = put(column, x, weight * memb[x, rows, :].astype(F32))
                column = put(column, LX + x, weight * syn[x, rows, :].astype(F32))
            columns[rows, :] = column

    def put(column, place, value):
        return jnp.where(lane == place, jnp.sum(value, axis=1, keepdims=True), column)

    for step in range(H // ROWS + 1):
        if step < H // ROWS:
            cells(step)
        if step >= 1:
            weights(step - 1)
    for half in range(2):
        lines = jnp.transpose(columns[half * LZ : (half + 1) * LZ, :])
        own_m, own_s, deep = lines[0:LX], lines[LX : 2 * LX], lines[3 * LX : 4 * LX]
        for c in range(3):
            total_z[c * LX : (c + 1) * LX, half * LZ : (half + 1) * LZ] = (
                MEMBRANE_COLOR[c] * own_m + SYNAPSE_COLOR[c] * own_s
            )
        total_z[3 * LX :, half * LZ : (half + 1) * LZ] = -deep


def shade_kernel(
    marks, inten, weight_x, weight_z, steep, hue, spot, along, tables, own_x, total_x, total_z,
    odd_x, face_a, face_b, even_x,
    keep, send, z_keep, z_send,
    pad, halo, left, dz, image, columns,
):
    core, zpos, gx = marks[0:1, :], marks[1:2, :], marks[2:3, :]
    lane_z = jnp.concatenate([zpos, zpos], axis=1)
    odd_z = lane_z & 1
    low = jnp.where(core == 0, odd_x[...].astype(F32), even_x[...].astype(F32))
    high = jnp.where(core == 0, even_x[...].astype(F32), odd_x[...].astype(F32))
    pad[0] = jnp.where(gx == 0, 0.0, low)
    pad[1] = jnp.where(gx == 63, 0.0, high)
    near = jnp.where(lane_z == 0, 0.0, jnp.where(odd_z == 0, face_b[...], face_a[...]))
    far = jnp.where(lane_z == 3, 0.0, jnp.where(odd_z == 0, face_a[...], face_b[...]))
    both = jnp.concatenate([near, far], axis=0).astype(BF16)
    halo[...] = mxu(both, as_bf16(iota((16, LZ), 0) == iota((16, LZ), 1)), TN).astype(BF16)
    k, n = iota((2 * LZ, LZ), 0), iota((2 * LZ, LZ), 1)
    up = ((k < LZ) & (k == n + 1)) | ((k >= LZ + LX) & (k < LZ + 2 * LX) & (n == LZ - 1))
    down = ((k < LZ) & (k == n - 1)) | ((k >= LZ) & (k < LZ + LX) & (n == 0))
    diff_z = (jnp.where(up, 1.0, 0.0) - jnp.where(down, 1.0, 0.0)).astype(BF16)
    lanes = iota((ROWS, LZ), 1)
    lane = iota((16, LZ), 1)
    first_half = iota((8, LZ), 0) < 4
    knots = [[tables[c, i] for i in range(2 if c + EARLY in ACROSS else 4)] for c in range(3 - EARLY)]

    def slopes(j):
        buf, base = j % 2, j * ROWS
        halo_rows = halo[base : base + ROWS, :]
        for x in range(LX):
            mine = jnp.where((lanes == x) | (lanes == LX + x), halo_rows, jnp.zeros_like(halo_rows))
            left[buf, x * ROWS : (x + 1) * ROWS, 0:LZ] = inten[x, base : base + ROWS, :]
            left[buf, x * ROWS : (x + 1) * ROWS, LZ:] = mine
        dz[buf] = mxu(left[buf], diff_z, NN)

    def cells(j, b):
        buf = j % 2
        rows = pl.ds(j * ROWS + b, 16)
        own_m, own_s = own_x[0, rows, :], own_x[1, rows, :]
        acc = [MEMBRANE_COLOR[c] * own_m + SYNAPSE_COLOR[c] * own_s for c in range(3)]
        column = jnp.zeros((16, LZ), F32)
        values = [pad[0, rows, :]] + [inten[x, rows, :].astype(F32) for x in range(LX)] + [pad[1, rows, :]]
        for x in range(LX):
            row = x * ROWS + b
            grad_x = values[x + 2] - values[x]
            grad_z = dz[buf, row : row + 16, :]
            norm = lax.rsqrt(grad_x * grad_x + (grad_z * grad_z + steep[x, rows, :]))
            lit_x = (0.3 / 0.7 + jnp.abs(grad_x) * norm) * weight_x[x, rows, :]
            lit_z = (0.3 / 0.7 + jnp.abs(grad_z) * norm) * weight_z[x, rows, :]
            index, frac = spot[x, rows, :], along[x, rows, :]
            for c in range(3):
                color = hue[c, x, rows, :] if c < EARLY else interpolate(knots[c - EARLY], index, frac)
                acc[c] = acc[c] + lit_x * color
                summed = jnp.sum(lit_z * color, axis=1, keepdims=True)
                column = jnp.where(lane == c * LX + x, summed, column)
        for c in range(3):
            image[c, rows, :] = acc[c]
        columns[rows, :] = column

    chunks = H // ROWS
    slopes(0)
    for j in range(chunks):
        for i, b in enumerate(range(0, ROWS, 16)):
            if i == 0 and j + 1 < chunks:
                slopes(j + 1)
            cells(j, b)
    swap = lambda v: pltpu.roll(v, 4, 0)
    for first in range(0, CHIPS, 8):
        ready = []
        for chip in range(first, first + 8):
            rows = pl.ds(8 * chip, 8)
            a, d, g = [image[c, rows, :] for c in range(3)]
            t = -total_x[rows, :]
            for i, (p, q) in enumerate(((a, d), (g, t))):
                crossed = swap(jnp.where(first_half, q, p))
                for_0 = jnp.where(first_half, p, crossed)
                for_1 = jnp.where(first_half, crossed, q)
                ready.append((keep, chip, i, jnp.where(core == 0, for_0, for_1)))
                ready.append((send, chip, i, jnp.where(core == 0, for_1, for_0)))
        for out, chip, i, value in ready:
            out[chip, 8 * i : 8 * i + 8, :] = value
    low, high = [
        total_z[:, half * LZ : (half + 1) * LZ]
        + jnp.where(
            iota((4 * LX, LZ), 0) < 3 * LX, jnp.transpose(columns[half * LZ : (half + 1) * LZ, :])[: 4 * LX], 0.0
        )
        for half in range(2)
    ]
    near_half = iota((4 * LX, LZ), 1) < ROWS
    outer = jnp.where(near_half, low, high)
    inner = pltpu.roll(jnp.where(near_half, high, low), ROWS, 1)
    edge = (zpos == 0) | (zpos == 3)
    z_keep[...] = jnp.where(edge, outer, inner)
    z_send[...] = jnp.where(edge, inner, outer)


def depth_rows(b):
    return jnp.where(iota((8, LZ), 0) < 4, pltpu.roll(b, 4, 0), b)


def z_merge(first, second):
    passed = jnp.exp2(-first[3 * LX :])
    rows = [first[c * LX : (c + 1) * LX] + passed * second[c * LX : (c + 1) * LX] for c in range(3)]
    return jnp.concatenate(rows + [first[3 * LX :] + second[3 * LX :]], axis=0)


def z_kernel(marks, z_mine, z_other, z_pair):
    even = (marks[1:2, :] & 1) == 0
    zm, zo = z_mine[...], z_other[...]
    z_pair[...] = z_merge(jnp.where(even, zm, zo), jnp.where(even, zo, zm))


def pair_kernel(marks, mine, other, code):
    core = marks[0:1, :]
    first_half = iota((8, LZ), 0) < 4
    for i in range(CHIPS):
        ma, mb = mine[i, 0:8, :], mine[i, 8:16, :]
        oa, ob = other[i, 0:8, :], other[i, 8:16, :]
        fa, fb = jnp.where(core == 0, ma, oa), jnp.where(core == 0, mb, ob)
        sa, sb = jnp.where(core == 0, oa, ma), jnp.where(core == 0, ob, mb)
        passed = jnp.exp2(-depth_rows(fb))
        a = fa + passed * sa
        b = fb + jnp.where(first_half, passed, 1.0) * sb
        v = jnp.concatenate([a, b], axis=0)
        q = jnp.log2(jnp.maximum(v, 2.0**-25)) * CODE_SCALE + (CODE_MID * CODE_SCALE)
        q = jnp.where(v > 2.0**-25, jnp.round(jnp.minimum(q, 32766.0)), -32768.0)
        code[i] = q.astype(jnp.int32).astype(jnp.int16)


def final_kernel(marks, code, z_mine, z_other, x_image, z_image):
    front = marks[1:2, :] < 2
    a = b = deep = jnp.zeros((8, LZ), F32)
    for i in range(CHIPS):
        q = code[i].astype(F32)
        v = jnp.exp2(q * (1.0 / CODE_SCALE) - CODE_MID)
        v = jnp.where(q < -32767.0, 0.0, v)
        passed = jnp.exp2(-deep)
        a = a + passed * v[0:8]
        b = b + passed * v[8:16]
        deep = deep + depth_rows(v[8:16])
    x_image[0] = a[0:4]
    x_image[1] = a[4:8]
    x_image[2] = b[0:4]
    x_image[3] = (1.0 - jnp.exp2(-deep))[0:4]

    zm, zo = z_mine[...], z_other[...]
    image = z_merge(jnp.where(front, zm, zo), jnp.where(front, zo, zm))
    image = jnp.where(front, image, pltpu.roll(image, ROWS, 1))[:, 0:ROWS]
    for c in range(3):
        z_image[c] = image[c * LX : (c + 1) * LX]
    z_image[3] = 1.0 - jnp.exp2(-image[3 * LX :])


def call(kernel, out_shape, scratch, cost, *operands, wide=False):
    specs = [
        pl.BlockSpec(memory_space=pl.ANY if wide and a.ndim == 3 else pltpu.VMEM)
        for a in operands
    ]
    return pl.pallas_call(
        kernel,
        out_shape=out_shape,
        in_specs=specs,
        out_specs=[pl.BlockSpec(memory_space=pltpu.VMEM)] * len(out_shape),
        scratch_shapes=scratch,
        compiler_params=pltpu.CompilerParams(vmem_limit_bytes=WIDE if wide else 32 * 2**20),
        cost_estimate=pl.CostEstimate(flops=cost, bytes_accessed=2**20, transcendentals=0),
    )(*operands)


LAYER, FACE = jax.ShapeDtypeStruct((H, LZ), BF16), jax.ShapeDtypeStruct((LX, H), F32)
BRICK = jax.ShapeDtypeStruct((LX, H, LZ), F32)
HALF = jax.ShapeDtypeStruct((CHIPS, 16, LZ), F32)
ZPART = jax.ShapeDtypeStruct((4 * LX, LZ), F32)
IMAGES = [jax.ShapeDtypeStruct((4, 4, LZ), F32), jax.ShapeDtypeStruct((4, LX, ROWS), F32)]
CODE = jax.ShapeDtypeStruct((CHIPS, 16, LZ), jnp.int16)


def faces(*operands):
    brick = jax.ShapeDtypeStruct((LX, H, LZ), BF16)
    outs = [LAYER, FACE, FACE, LAYER, brick, brick, brick]
    return call(faces_kernel, outs, [pltpu.SemaphoreType.DMA((3,))], 10**6, *operands, wide=True)


def depths(intensity, membrane, synapse, transfer, occupancy):
    outs = [BRICK] * 3 + [jax.ShapeDtypeStruct((EARLY, LX, H, LZ), F32)] + [
        jax.ShapeDtypeStruct((LX, H, LZ), jnp.int32),
        BRICK,
        jax.ShapeDtypeStruct((3 - EARLY, 4, 8, LZ), F32),
        jax.ShapeDtypeStruct((2, H, LZ), F32),
        jax.ShapeDtypeStruct((H, LZ), F32),
        jax.ShapeDtypeStruct((4 * LX, H), F32),
    ]
    scratch = [
        pltpu.VMEM((H // 8, LZ), F32),
        pltpu.VMEM((2, LX * ROWS, LZ), F32),
        pltpu.VMEM((2, LX * ROWS, LZ), F32),
        pltpu.VMEM((2, LX * ROWS, 2 * LZ), BF16),
        pltpu.VMEM((H, LZ), F32),
    ]
    return call(depth_kernel, outs, scratch, 10**8, intensity, membrane, synapse, transfer, occupancy)


def shades(*operands):
    scratch = [
        pltpu.VMEM((2, H, LZ), F32),
        pltpu.VMEM((H, LZ), BF16),
        pltpu.VMEM((2, LX * ROWS, 2 * LZ), BF16),
        pltpu.VMEM((2, LX * ROWS, LZ), F32),
        pltpu.VMEM((3, H, LZ), F32),
        pltpu.VMEM((H, LZ), F32),
    ]
    return call(shade_kernel, [HALF, HALF, ZPART, ZPART], scratch, 10**8, *operands)


def body(intensity, membrane, synapse, transfer, occupancy):
    gx = ("z", "y", "core")
    place = jnp.stack([lax.axis_index("core"), lax.axis_index("x"), lax.axis_index(gx)]).astype(jnp.int32)
    marks = jnp.broadcast_to(jnp.pad(place, (0, 5))[:, None], (8, LZ))
    odd_x, face_a, face_b, even_x, intensity, membrane, synapse = faces(marks, intensity, membrane, synapse)
    even = [p for i in range(0, 64, 2) for p in ((i, i + 1), (i + 1, i))]
    odd = [p for i in range(1, 64, 2) for p in ((i, (i + 1) % 64), ((i + 1) % 64, i))]
    odd_x = lax.ppermute(odd_x, gx, odd)
    face_a = lax.ppermute(face_a, "x", [(0, 1), (1, 0), (2, 3), (3, 2)])
    face_b = lax.ppermute(face_b, "x", [(1, 2), (2, 1), (3, 0), (0, 3)])
    even_x = lax.ppermute(even_x, gx, even)
    transfer = jnp.pad(transfer, ((0, 4), (0, LZ - KNOTS)))
    deep = depths(intensity, membrane, synapse, transfer, occupancy)
    keep, send, z_keep, z_send = shades(
        marks, intensity, *deep, odd_x, face_a, face_b, even_x
    )
    other = lax.ppermute(send, "core", [(0, 1), (1, 0)])
    z_other = lax.ppermute(z_send, "x", [(0, 1), (1, 0), (2, 3), (3, 2)])
    (code,) = call(pair_kernel, [CODE], [], 10**6, marks, keep, other)
    (z_pair,) = call(z_kernel, [ZPART], [], 10**11, marks, z_keep, z_other)
    z_other = lax.ppermute(z_pair, "x", [(0, 3), (3, 0), (1, 2), (2, 1)])
    code = lax.all_to_all(code, ("z", "y"), split_axis=0, concat_axis=0, tiled=True)
    return tuple(call(final_kernel, IMAGES, [], 10**6, marks, code, z_pair, z_other))


def solution(mesh):
    split_mesh = Mesh(mesh.devices.reshape(8, 4, 2, 4), ("z", "y", "core", "x"))
    gx = ("z", "y", "core")
    brick = P(gx, None, "x")
    return jax.shard_map(
        body,
        mesh=split_mesh,
        in_specs=(brick, brick, brick, P(), brick),
        out_specs=(P(None, gx, "x"), P(None, gx, "x")),
        check_vma=False,
    )
```

```python
import jax
import jax.numpy as jnp
from jax import lax
from jax.experimental import pallas as pl
from jax.experimental.pallas import tpu as pltpu
from jax.sharding import Mesh, PartitionSpec as P

MEMBRANE_COLOR = (0.9, 0.2, 0.1)
SYNAPSE_COLOR = (0.1, 0.8, 0.3)
LX, H, LZ = 8, 256, 128
KNOTS = 16
ROWS = 64
CHIPS = 32
EARLY = 1
ACROSS = ()
WIDE = 52 * 2**20
F32, BF16 = jnp.float32, jnp.bfloat16
CODE_SCALE = 32760.0 / 12.0
CODE_MID = 13.0
LN2 = 0.6931471805599453
NN = (((1,), (0,)), ((), ()))
NT = (((1,), (1,)), ((), ()))
TN = (((0,), (0,)), ((), ()))


def mxu(a, b, dims):
    return lax.dot_general(a, b, dims, preferred_element_type=F32)


def iota(shape, dim):
    return lax.broadcasted_iota(jnp.int32, shape, dim)


def as_bf16(mask, value=1.0):
    return jnp.where(mask, value, 0.0).astype(BF16)


def split(value):
    high = value.astype(BF16)
    return high, (value - high.astype(F32)).astype(BF16)


def faces_kernel(
    marks, inten_hbm, memb_hbm, syn_hbm,
    odd_x, face_a, face_b, even_x, intensity, memb, syn, sems,
):
    pairs = ((inten_hbm, intensity), (memb_hbm, memb), (syn_hbm, syn))
    copies = [pltpu.make_async_copy(a, b, sems.at[i]) for i, (a, b) in enumerate(pairs)]
    for copy in copies:
        copy.start()
    copies[0].wait()
    core, odd_z = marks[0:1, :], marks[1:2, :] & 1
    first, last = intensity[0].astype(F32), intensity[LX - 1].astype(F32)
    even_x[...] = jnp.where(core == 0, last, first).astype(BF16)
    odd_x[...] = jnp.where(core == 0, first, last).astype(BF16)
    row, lane = iota((16, LZ), 0), iota((16, LZ), 1)
    lane_a = jnp.where(odd_z == 0, LZ - 1, 0)
    wanted = jnp.where(row < LX, lane_a, LZ - 1 - lane_a)
    total = jnp.zeros((16, H), F32)
    for x in range(LX):
        pick = as_bf16((row % LX == x) & (lane == wanted))
        total = total + mxu(pick, intensity[x], NT)
    face_a[...] = total[:LX]
    face_b[...] = total[LX:]
    for copy in copies[1:]:
        copy.wait()


def lookup(value):
    t = jnp.clip(value, 0.0, 1.0) * (KNOTS - 1.0)
    index = jnp.minimum(t.astype(jnp.int32), KNOTS - 2)
    return index, t - index.astype(F32)


def gather(table, index, dim):
    numbers = lax.GatherDimensionNumbers(
        offset_dims=(), collapsed_slice_dims=(dim,), start_index_map=(dim,),
        operand_batching_dims=(1 - dim,), start_indices_batching_dims=(1 - dim,),
    )
    return lax.gather(
        table, index[..., None], numbers, (1, 1), mode=lax.GatherScatterMode.PROMISE_IN_BOUNDS
    )


def knot_table(transfer, channel, factor, across):
    knots = transfer[...] * factor
    steps = pltpu.roll(knots, LZ - 1, 1) - knots
    out = []
    for values in (knots, steps):
        line = jnp.broadcast_to(values[channel : channel + 1], (8, LZ))
        if across:
            out.append(line)
            continue
        for first in (0, 8):
            own = jnp.where(iota((8, LZ), 1) == iota((8, LZ), 0) + first, line, 0.0)
            out.append(jnp.broadcast_to(jnp.sum(own, axis=1, keepdims=True), (8, LZ)))
    return out


def interpolate(tables, index, frac):
    halves = []
    for h in (slice(0, 8), slice(8, 16)):
        if len(tables) == 2:
            first, step = gather(tables[0], index[h], 1), gather(tables[1], index[h], 1)
        else:
            row, upper = index[h] & 7, index[h] >= 8
            first = jnp.where(upper, gather(tables[1], row, 0), gather(tables[0], row, 0))
            step = jnp.where(upper, gather(tables[3], row, 0), gather(tables[2], row, 0))
        halves.append(first + frac[h] * step)
    return jnp.concatenate(halves, axis=0)


def depth_kernel(
    inten, memb, syn, transfer, occ,
    weight_x, weight_z, steep, hue, spot, along, tables, own_x, total_x, total_z,
    occ_rows, sigma, prefix, parts, columns,
):
    scale = -2.0 / (LX * 64) / LN2
    dense = knot_table(transfer, 3, scale, False)
    knots = [knot_table(transfer, c, 0.7, c in ACROSS) for c in range(3)]
    for c in range(EARLY, 3):
        for i, table in enumerate(knots[c]):
            tables[c - EARLY, i] = table
    spread = as_bf16(iota((KNOTS, LZ), 1) // 8 == iota((KNOTS, LZ), 0))
    occ_rows[...] = mxu(occ[0].astype(F32).astype(BF16), spread, NN)
    r, k = iota((H, H), 0), iota((H, H), 1)
    diff_y = (jnp.where(k == r + 1, 1.0, 0.0) - jnp.where(k == r - 1, 1.0, 0.0)).astype(BF16)
    k, n = iota((2 * LZ, LZ), 0), iota((2 * LZ, LZ), 1)
    before = as_bf16(k % LZ < n)
    lane = iota((16, LZ), 1)
    for x in range(LX):
        grad_y = mxu(diff_y, inten[x], NN)
        steep[x] = grad_y * grad_y + 1.0
    def cells(j):
        buf = j % 2
        for b in range(0, ROWS, 16):
            rows = pl.ds(j * ROWS + b, 16)
            block = (j * ROWS + b) // 8
            mask = jnp.concatenate(
                [jnp.broadcast_to(occ_rows[block + i : block + i + 1, :], (8, LZ)) for i in range(2)], axis=0
            )
            total = jnp.zeros((16, LZ), F32)
            trans = jnp.ones((16, LZ), F32)
            own_m = jnp.zeros((16, LZ), F32)
            own_s = jnp.zeros((16, LZ), F32)
            column = jnp.zeros((16, LZ), F32)
            for x in range(LX):
                index, frac = lookup(inten[x, rows, :].astype(F32))
                spot[x, rows, :] = index
                along[x, rows, :] = frac
                for c in range(EARLY):
                    hue[c, x, rows, :] = interpolate(knots[c], index, frac)
                mem = memb[x, rows, :].astype(F32)
                sy = syn[x, rows, :].astype(F32)
                depth = interpolate(dense, index, frac) + mem * (1.5 * scale)
                depth = (depth + sy * (0.5 * scale)) * mask
                high, low = split(depth)
                row = x * ROWS + b
                parts[buf, row : row + 16, 0:LZ] = high
                parts[buf, row : row + 16, LZ:] = low
                passed = jnp.exp2(depth)
                alpha = 1.0 - passed
                sigma[buf, row : row + 16, :] = alpha
                weight = trans * alpha
                weight_x[x, rows, :] = weight
                own_m = own_m + weight * mem
                own_s = own_s + weight * sy
                trans = trans * passed
                total = total + depth
                column = put(column, 3 * LX + x, depth)
            columns[rows, :] = column
            total_x[rows, :] = total
            own_x[0, rows, :] = own_m
            own_x[1, rows, :] = own_s
        prefix[buf] = mxu(parts[buf], before, NN)

    def weights(j):
        buf = j % 2
        for b in range(0, ROWS, 16):
            rows = pl.ds(j * ROWS + b, 16)
            column = columns[rows, :]
            for x in range(LX):
                here = slice(x * ROWS + b, x * ROWS + b + 16)
                weight = jnp.exp2(prefix[buf, here, :]) * sigma[buf, here, :]
                weight_z[x, rows, :] = weight
                column = put(column, x, weight * memb[x, rows, :].astype(F32))
                column = put(column, LX + x, weight * syn[x, rows, :].astype(F32))
            columns[rows, :] = column

    def put(column, place, value):
        return jnp.where(lane == place, jnp.sum(value, axis=1, keepdims=True), column)

    for step in range(H // ROWS + 1):
        if step < H // ROWS:
            cells(step)
        if step >= 1:
            weights(step - 1)
    for half in range(2):
        lines = jnp.transpose(columns[half * LZ : (half + 1) * LZ, :])
        own_m, own_s, deep = lines[0:LX], lines[LX : 2 * LX], lines[3 * LX : 4 * LX]
        for c in range(3):
            total_z[c * LX : (c + 1) * LX, half * LZ : (half + 1) * LZ] = (
                MEMBRANE_COLOR[c] * own_m + SYNAPSE_COLOR[c] * own_s
            )
        total_z[3 * LX :, half * LZ : (half + 1) * LZ] = -deep


def shade_kernel(
    marks, inten, weight_x, weight_z, steep, hue, spot, along, tables, own_x, total_x, total_z,
    odd_x, face_a, face_b, even_x,
    keep, send, z_keep, z_send,
    pad, halo, left, dz, image, columns,
):
    core, zpos, gx = marks[0:1, :], marks[1:2, :], marks[2:3, :]
    lane_z = jnp.concatenate([zpos, zpos], axis=1)
    odd_z = lane_z & 1
    low = jnp.where(core == 0, odd_x[...].astype(F32), even_x[...].astype(F32))
    high = jnp.where(core == 0, even_x[...].astype(F32), odd_x[...].astype(F32))
    pad[0] = jnp.where(gx == 0, 0.0, low)
    pad[1] = jnp.where(gx == 63, 0.0, high)
    near = jnp.where(lane_z == 0, 0.0, jnp.where(odd_z == 0, face_b[...], face_a[...]))
    far = jnp.where(lane_z == 3, 0.0, jnp.where(odd_z == 0, face_a[...], face_b[...]))
    both = jnp.concatenate([near, far], axis=0).astype(BF16)
    halo[...] = mxu(both, as_bf16(iota((16, LZ), 0) == iota((16, LZ), 1)), TN).astype(BF16)
    k, n = iota((2 * LZ, LZ), 0), iota((2 * LZ, LZ), 1)
    up = ((k < LZ) & (k == n + 1)) | ((k >= LZ + LX) & (k < LZ + 2 * LX) & (n == LZ - 1))
    down = ((k < LZ) & (k == n - 1)) | ((k >= LZ) & (k < LZ + LX) & (n == 0))
    diff_z = (jnp.where(up, 1.0, 0.0) - jnp.where(down, 1.0, 0.0)).astype(BF16)
    lanes = iota((ROWS, LZ), 1)
    lane = iota((16, LZ), 1)
    first_half = iota((8, LZ), 0) < 4
    knots = [[tables[c, i] for i in range(2 if c + EARLY in ACROSS else 4)] for c in range(3 - EARLY)]

    def slopes(j):
        buf, base = j % 2, j * ROWS
        halo_rows = halo[base : base + ROWS, :]
        for x in range(LX):
            mine = jnp.where((lanes == x) | (lanes == LX + x), halo_rows, jnp.zeros_like(halo_rows))
            left[buf, x * ROWS : (x + 1) * ROWS, 0:LZ] = inten[x, base : base + ROWS, :]
            left[buf, x * ROWS : (x + 1) * ROWS, LZ:] = mine
        dz[buf] = mxu(left[buf], diff_z, NN)

    def cells(j, b):
        buf = j % 2
        rows = pl.ds(j * ROWS + b, 16)
        own_m, own_s = own_x[0, rows, :], own_x[1, rows, :]
        acc = [MEMBRANE_COLOR[c] * own_m + SYNAPSE_COLOR[c] * own_s for c in range(3)]
        column = jnp.zeros((16, LZ), F32)
        values = [pad[0, rows, :]] + [inten[x, rows, :].astype(F32) for x in range(LX)] + [pad[1, rows, :]]
        for x in range(LX):
            row = x * ROWS + b
            grad_x = values[x + 2] - values[x]
            grad_z = dz[buf, row : row + 16, :]
            norm = lax.rsqrt(grad_x * grad_x + (grad_z * grad_z + steep[x, rows, :]))
            lit_x = (0.3 / 0.7 + jnp.abs(grad_x) * norm) * weight_x[x, rows, :]
            lit_z = (0.3 / 0.7 + jnp.abs(grad_z) * norm) * weight_z[x, rows, :]
            index, frac = spot[x, rows, :], along[x, rows, :]
            for c in range(3):
                color = hue[c, x, rows, :] if c < EARLY else interpolate(knots[c - EARLY], index, frac)
                acc[c] = acc[c] + lit_x * color
                summed = jnp.sum(lit_z * color, axis=1, keepdims=True)
                column = jnp.where(lane == c * LX + x, summed, column)
        for c in range(3):
            image[c, rows, :] = acc[c]
        columns[rows, :] = column

    chunks = H // ROWS
    slopes(0)
    for j in range(chunks):
        for i, b in enumerate(range(0, ROWS, 16)):
            if i == 0 and j + 1 < chunks:
                slopes(j + 1)
            cells(j, b)
    swap = lambda v: pltpu.roll(v, 4, 0)
    for first in range(0, CHIPS, 8):
        ready = []
        for chip in range(first, first + 8):
            rows = pl.ds(8 * chip, 8)
            a, d, g = [image[c, rows, :] for c in range(3)]
            t = -total_x[rows, :]
            for i, (p, q) in enumerate(((a, d), (g, t))):
                crossed = swap(jnp.where(first_half, q, p))
                for_0 = jnp.where(first_half, p, crossed)
                for_1 = jnp.where(first_half, crossed, q)
                ready.append((keep, chip, i, jnp.where(core == 0, for_0, for_1)))
                ready.append((send, chip, i, jnp.where(core == 0, for_1, for_0)))
        for out, chip, i, value in ready:
            out[chip, 8 * i : 8 * i + 8, :] = value
    low, high = [
        total_z[:, half * LZ : (half + 1) * LZ]
        + jnp.where(
            iota((4 * LX, LZ), 0) < 3 * LX, jnp.transpose(columns[half * LZ : (half + 1) * LZ, :])[: 4 * LX], 0.0
        )
        for half in range(2)
    ]
    near_half = iota((4 * LX, LZ), 1) < ROWS
    outer = jnp.where(near_half, low, high)
    inner = pltpu.roll(jnp.where(near_half, high, low), ROWS, 1)
    edge = (zpos == 0) | (zpos == 3)
    z_keep[...] = jnp.where(edge, outer, inner)
    z_send[...] = jnp.where(edge, inner, outer)


def depth_rows(b):
    return jnp.where(iota((8, LZ), 0) < 4, pltpu.roll(b, 4, 0), b)


def z_merge(first, second):
    passed = jnp.exp2(-first[3 * LX :])
    rows = [first[c * LX : (c + 1) * LX] + passed * second[c * LX : (c + 1) * LX] for c in range(3)]
    return jnp.concatenate(rows + [first[3 * LX :] + second[3 * LX :]], axis=0)


def z_kernel(marks, z_mine, z_other, z_pair):
    even = (marks[1:2, :] & 1) == 0
    zm, zo = z_mine[...], z_other[...]
    z_pair[...] = z_merge(jnp.where(even, zm, zo), jnp.where(even, zo, zm))


def pair_kernel(marks, mine, other, code_out, code, sems):
    core = marks[0:1, :]
    first_half = iota((8, LZ), 0) < 4
    copies = []
    for i in range(CHIPS):
        ma, mb = mine[i, 0:8, :], mine[i, 8:16, :]
        oa, ob = other[i, 0:8, :], other[i, 8:16, :]
        fa, fb = jnp.where(core == 0, ma, oa), jnp.where(core == 0, mb, ob)
        sa, sb = jnp.where(core == 0, oa, ma), jnp.where(core == 0, ob, mb)
        passed = jnp.exp2(-depth_rows(fb))
        a = fa + passed * sa
        b = fb + jnp.where(first_half, passed, 1.0) * sb
        v = jnp.concatenate([a, b], axis=0)
        q = jnp.log2(jnp.maximum(v, 2.0**-25)) * CODE_SCALE + (CODE_MID * CODE_SCALE)
        q = jnp.where(v > 2.0**-25, jnp.round(jnp.minimum(q, 32766.0)), -32768.0)
        code[i] = q.astype(jnp.int32).astype(jnp.int16)
        if i % 8 == 7:
            part = pl.ds(i - 7, 8)
            copies.append(pltpu.make_async_copy(code.at[part], code_out.at[part], sems.at[i // 8]))
            copies[-1].start()
    for copy in copies:
        copy.wait()


def final_kernel(marks, code, z_mine, z_other, x_image, z_image):
    front = marks[1:2, :] < 2
    a = b = deep = jnp.zeros((8, LZ), F32)
    for i in range(CHIPS):
        q = code[i].astype(F32)
        v = jnp.exp2(q * (1.0 / CODE_SCALE) - CODE_MID)
        v = jnp.where(q < -32767.0, 0.0, v)
        passed = jnp.exp2(-deep)
        a = a + passed * v[0:8]
        b = b + passed * v[8:16]
        deep = deep + depth_rows(v[8:16])
    x_image[0] = a[0:4]
    x_image[1] = a[4:8]
    x_image[2] = b[0:4]
    x_image[3] = (1.0 - jnp.exp2(-deep))[0:4]

    zm, zo = z_mine[...], z_other[...]
    image = z_merge(jnp.where(front, zm, zo), jnp.where(front, zo, zm))
    image = jnp.where(front, image, pltpu.roll(image, ROWS, 1))[:, 0:ROWS]
    for c in range(3):
        z_image[c] = image[c * LX : (c + 1) * LX]
    z_image[3] = 1.0 - jnp.exp2(-image[3 * LX :])


def call(kernel, out_shape, scratch, cost, *operands, wide=False, results=pltpu.VMEM):
    specs = [
        pl.BlockSpec(memory_space=pl.ANY if wide and a.ndim == 3 else pltpu.VMEM)
        for a in operands
    ]
    return pl.pallas_call(
        kernel,
        out_shape=out_shape,
        in_specs=specs,
        out_specs=[pl.BlockSpec(memory_space=results)] * len(out_shape),
        scratch_shapes=scratch,
        compiler_params=pltpu.CompilerParams(vmem_limit_bytes=WIDE if wide else 32 * 2**20),
        cost_estimate=pl.CostEstimate(flops=cost, bytes_accessed=2**20, transcendentals=0),
    )(*operands)


LAYER, FACE = jax.ShapeDtypeStruct((H, LZ), BF16), jax.ShapeDtypeStruct((LX, H), F32)
BRICK = jax.ShapeDtypeStruct((LX, H, LZ), F32)
HALF = jax.ShapeDtypeStruct((CHIPS, 16, LZ), F32)
ZPART = jax.ShapeDtypeStruct((4 * LX, LZ), F32)
IMAGES = [jax.ShapeDtypeStruct((4, 4, LZ), F32), jax.ShapeDtypeStruct((4, LX, ROWS), F32)]
CODE = jax.ShapeDtypeStruct((CHIPS, 16, LZ), jnp.int16)


def faces(*operands):
    brick = jax.ShapeDtypeStruct((LX, H, LZ), BF16)
    outs = [LAYER, FACE, FACE, LAYER, brick, brick, brick]
    return call(faces_kernel, outs, [pltpu.SemaphoreType.DMA((3,))], 10**6, *operands, wide=True)


def depths(intensity, membrane, synapse, transfer, occupancy):
    outs = [BRICK] * 3 + [jax.ShapeDtypeStruct((EARLY, LX, H, LZ), F32)] + [
        jax.ShapeDtypeStruct((LX, H, LZ), jnp.int32),
        BRICK,
        jax.ShapeDtypeStruct((3 - EARLY, 4, 8, LZ), F32),
        jax.ShapeDtypeStruct((2, H, LZ), F32),
        jax.ShapeDtypeStruct((H, LZ), F32),
        jax.ShapeDtypeStruct((4 * LX, H), F32),
    ]
    scratch = [
        pltpu.VMEM((H // 8, LZ), F32),
        pltpu.VMEM((2, LX * ROWS, LZ), F32),
        pltpu.VMEM((2, LX * ROWS, LZ), F32),
        pltpu.VMEM((2, LX * ROWS, 2 * LZ), BF16),
        pltpu.VMEM((H, LZ), F32),
    ]
    return call(depth_kernel, outs, scratch, 10**8, intensity, membrane, synapse, transfer, occupancy)


def shades(*operands):
    scratch = [
        pltpu.VMEM((2, H, LZ), F32),
        pltpu.VMEM((H, LZ), BF16),
        pltpu.VMEM((2, LX * ROWS, 2 * LZ), BF16),
        pltpu.VMEM((2, LX * ROWS, LZ), F32),
        pltpu.VMEM((3, H, LZ), F32),
        pltpu.VMEM((H, LZ), F32),
    ]
    return call(shade_kernel, [HALF, HALF, ZPART, ZPART], scratch, 10**8, *operands)


def body(intensity, membrane, synapse, transfer, occupancy):
    gx = ("z", "y", "core")
    place = jnp.stack([lax.axis_index("core"), lax.axis_index("x"), lax.axis_index(gx)]).astype(jnp.int32)
    marks = jnp.broadcast_to(jnp.pad(place, (0, 5))[:, None], (8, LZ))
    odd_x, face_a, face_b, even_x, intensity, membrane, synapse = faces(marks, intensity, membrane, synapse)
    even = [p for i in range(0, 64, 2) for p in ((i, i + 1), (i + 1, i))]
    odd = [p for i in range(1, 64, 2) for p in ((i, (i + 1) % 64), ((i + 1) % 64, i))]
    odd_x = lax.ppermute(odd_x, gx, odd)
    face_a = lax.ppermute(face_a, "x", [(0, 1), (1, 0), (2, 3), (3, 2)])
    face_b = lax.ppermute(face_b, "x", [(1, 2), (2, 1), (3, 0), (0, 3)])
    even_x = lax.ppermute(even_x, gx, even)
    transfer = jnp.pad(transfer, ((0, 4), (0, LZ - KNOTS)))
    deep = depths(intensity, membrane, synapse, transfer, occupancy)
    keep, send, z_keep, z_send = shades(
        marks, intensity, *deep, odd_x, face_a, face_b, even_x
    )
    other = lax.ppermute(send, "core", [(0, 1), (1, 0)])
    z_other = lax.ppermute(z_send, "x", [(0, 1), (1, 0), (2, 3), (3, 2)])
    scratch = [pltpu.VMEM((CHIPS, 16, LZ), jnp.int16), pltpu.SemaphoreType.DMA((4,))]
    (code,) = call(pair_kernel, [CODE], scratch, 10**6, marks, keep, other, results=pl.ANY)
    (z_pair,) = call(z_kernel, [ZPART], [], 10**11, marks, z_keep, z_other)
    z_other = lax.ppermute(z_pair, "x", [(0, 3), (3, 0), (1, 2), (2, 1)])
    code = lax.all_to_all(code, ("z", "y"), split_axis=0, concat_axis=0, tiled=True)
    return tuple(call(final_kernel, IMAGES, [], 10**6, marks, code, z_pair, z_other))


def solution(mesh):
    split_mesh = Mesh(mesh.devices.reshape(8, 4, 2, 4), ("z", "y", "core", "x"))
    gx = ("z", "y", "core")
    brick = P(gx, None, "x")
    return jax.shard_map(
        body,
        mesh=split_mesh,
        in_specs=(brick, brick, brick, P(), brick),
        out_specs=(P(None, gx, "x"), P(None, gx, "x")),
        check_vma=False,
    )
```
